256 devices in a mesh: batch: 32 (over y_lo, z, core), tensor: 8 (over x, y_hi).
Axes of the slice: x: 4, y: 4 (y_hi: 2, y_lo: 2; y = y_hi * 2 + y_lo), z: 8, core: 2. Of those that a mesh axis runs over, the one named last changes fastest.
Arguments:
- queries: bfloat16 [128, 8192], P('batch', 'tensor'), may hold values from -80 to 80
- fresh_key_heads: bfloat16 [128, 1024], P('batch', 'tensor'), may hold values from -6 to 6
- fresh_value_heads: bfloat16 [128, 1024], P('batch', 'tensor'), may hold values from -6 to 6
- cached_keys: bfloat16 [128, 8, 4096, 128], P('batch', 'tensor'), may hold values from -6 to 6
- value_cache_rows: bfloat16 [128, 8, 4096, 128], P('batch', 'tensor'), may hold values from -6 to 6
- lengths: int32 [128], P('batch'), may hold values from 2 to 4096, as said below
- residual: bfloat16 [128, 5120], P('batch', 'tensor'), may hold values from -6 to 6
- sectioned_rows: bfloat16 [32, 256, 5120], P('batch', 'tensor'), may hold values from -0.5 to 0.5
- owners: int32 [32], replicated, may hold values from 0 to 31, each once
- norm_gain: bfloat16 [5120], P('tensor'), may hold values from 0.5 to 1.5
Outputs:
- updated_stream: bfloat16 [128, 5120], P('batch', 'tensor')
- normed_stream: bfloat16 [128, 5120], P('batch', 'tensor')
The draws below stay inside these ranges and needn't reach their ends.
Inputs may be any that keep to these rules, and one draw needn't show every extreme that they name: `lengths`: every sequence has at least two valid positions; some sequence fills all 4096. `owners`: each batch index owns exactly one piece.
All inputs are finite; a program needn't handle non-finite values.
Results may differ from the reference program's by a relative error of at most 0.018.
Values may be sent and summed in bfloat16 or wider, within the bound.
A program may use at most 64 MiB of HBM per device.

```python
import jax
import jax.numpy as jnp
from jax import lax

D = 5120
QUERY_HEADS = 64
KEY_VALUE_HEADS = 8
HEAD_SIZE = 128
CACHE_POSITIONS = 4096
SEQUENCE_COUNT = 128
PIECES = 32
N_TENSOR = 8


def anchors(key):
    base_offset = jnp.clip(jax.random.normal(jax.random.fold_in(key, 11), (SEQUENCE_COUNT, KEY_VALUE_HEADS, HEAD_SIZE), jnp.float32), -3.0, 3.0)
    spare_slot = jnp.clip(jax.random.normal(jax.random.fold_in(key, 12), (SEQUENCE_COUNT, KEY_VALUE_HEADS, HEAD_SIZE), jnp.float32), -3.0, 3.0)
    return (base_offset, spare_slot)


def draw_cached_keys(key, part):
    base_offset, spare_slot = anchors(key)
    key = jax.random.fold_in(key, 1)
    field_name = jnp.clip(jax.random.normal(key, (SEQUENCE_COUNT, KEY_VALUE_HEADS, CACHE_POSITIONS, HEAD_SIZE), jnp.float32), -6.0, 6.0)
    second = spare_slot
    field_name = field_name.at[:, :, 0, :].set(base_offset).at[:, :, 1, :].set(second)
    return field_name.astype(jnp.bfloat16)


def draw_queries(key, part):
    key = jax.random.fold_in(key, 2)
    head_group = QUERY_HEADS // KEY_VALUE_HEADS
    drawn_result = jnp.clip(jax.random.normal(key, (SEQUENCE_COUNT, KEY_VALUE_HEADS, head_group, HEAD_SIZE), jnp.float32), -6.0, 6.0)
    return drawn_result.reshape(SEQUENCE_COUNT, QUERY_HEADS * HEAD_SIZE).astype(jnp.bfloat16)


def draw_lengths(key, part):
    key = jax.random.fold_in(key, 3)
    values = jax.random.randint(key, (SEQUENCE_COUNT,), 2, CACHE_POSITIONS + 1)
    spot = jax.random.randint(jax.random.fold_in(key, 1), (), 0, SEQUENCE_COUNT)
    return values.at[spot].set(CACHE_POSITIONS).astype(jnp.int32)


def draw_residual(key, part):
    key = jax.random.fold_in(key, 4)
    ramp = 1.0 + 2.0 * jnp.arange(D, dtype=jnp.float32) / (D - 1)
    values = jnp.clip(jax.random.normal(key, (SEQUENCE_COUNT, D), jnp.float32), -6.0, 6.0)
    return (0.3 * values * ramp[None, :]).astype(jnp.bfloat16)


def steps_of(stream_key, dims, cuts, low, high):
    level, own = 1.0, jax.random.fold_in(stream_key, 6)
    for axis_at, blocks in cuts:
        steps = jnp.exp(jax.random.uniform(jax.random.fold_in(own, axis_at), (blocks,), jnp.float32, low / len(cuts), high / len(cuts)))
        level = level * jnp.repeat(steps, dims[axis_at] // blocks).reshape([-1 if axis == axis_at else 1 for axis in range(len(dims))])
    return level


def bell_draw(key, shape, scale, most, cuts=(), kind=jnp.bfloat16):
    array = jax.random.normal(key, shape, jnp.float32) * scale
    if len(cuts) > 0:
        array = steps_of(key, shape, cuts, -0.22, 0.18) * array
    return jnp.clip(array, min=-most, max=most).astype(kind)


def setup_inputs(seed: int = 0) -> dict:
    key_of = jax.random.split(jax.random.key(seed), 11)
    queries = draw_queries(jax.random.fold_in(key_of[10], 71), 0)
    fresh_key_heads = bell_draw(key_of[1], (SEQUENCE_COUNT, KEY_VALUE_HEADS * HEAD_SIZE), 1.0, 6.0, ((0, 32), (1, 8)))
    fresh_value_heads = bell_draw(key_of[2], (SEQUENCE_COUNT, KEY_VALUE_HEADS * HEAD_SIZE), 1.0, 6.0, ((0, 32), (1, 8)))
    cached_keys = draw_cached_keys(jax.random.fold_in(key_of[10], 71), 0)
    value_cache_rows = bell_draw(key_of[4], (SEQUENCE_COUNT, KEY_VALUE_HEADS, CACHE_POSITIONS, HEAD_SIZE), 1.0, 6.0, ((0, 32), (1, 8)))
    lengths = draw_lengths(jax.random.fold_in(key_of[10], 71), 0)
    residual = draw_residual(jax.random.fold_in(key_of[10], 71), 0)
    sectioned_rows = bell_draw(key_of[7], (PIECES, QUERY_HEADS * HEAD_SIZE // PIECES, D), HEAD_SIZE ** -0.5, 0.5, ((0, 32), (1, 8)))
    owners = jax.random.permutation(key_of[8], PIECES).astype(jnp.int32)
    norm_gain = jnp.clip(1.0 + 0.1 * jax.random.normal(key_of[9], (D,), jnp.float32), 0.5, 1.5).astype(jnp.bfloat16)
    return {"queries": queries, "fresh_key_heads": fresh_key_heads, "fresh_value_heads": fresh_value_heads, "cached_keys": cached_keys, "value_cache_rows": value_cache_rows, "lengths": lengths, "residual": residual, "sectioned_rows": sectioned_rows, "owners": owners, "norm_gain": norm_gain}


def reference(queries, fresh_key_heads, fresh_value_heads, cached_keys, value_cache_rows, lengths, residual, sectioned_rows, owners, norm_gain):
    head_group = QUERY_HEADS // KEY_VALUE_HEADS
    score_scale = HEAD_SIZE ** (-0.5)
    highest_score = lax.Precision.HIGHEST

    def one_sequence(items):
        query_vector, key_vector, value_vector, keys, values, length = items
        head_count = query_vector.astype(jnp.float32).reshape(KEY_VALUE_HEADS, head_group, HEAD_SIZE)
        scores = jnp.einsum('kgd,kld->kgl', head_count, keys.astype(jnp.float32), precision=highest_score) * score_scale
        valid = jnp.arange(CACHE_POSITIONS) < length
        scores = jnp.where(valid[None, None, :], scores, -1e+30)
        own_piece = jnp.einsum('ozv,ov->oz', head_count, key_vector.astype(jnp.float32).reshape(KEY_VALUE_HEADS, HEAD_SIZE), precision=highest_score) * score_scale
        top = jnp.maximum(lax.optimization_barrier(jnp.max(scores, axis=-1)), own_piece)
        probs = jnp.exp(scores - top[..., None])
        own_probability = jnp.exp(own_piece - top)
        total = lax.optimization_barrier(jnp.sum(probs, axis=-1)) + own_probability
        mixed_values = jnp.einsum('kgl,kld->kgd', probs.astype(jnp.bfloat16).astype(jnp.float32), values.astype(jnp.float32), precision=highest_score)
        mixed_values = mixed_values + own_probability.astype(jnp.bfloat16).astype(jnp.float32)[..., None] * value_vector.astype(jnp.float32).reshape(KEY_VALUE_HEADS, 1, HEAD_SIZE)
        return (mixed_values / total[..., None]).astype(jnp.bfloat16).reshape(QUERY_HEADS * HEAD_SIZE)
    attended = lax.map(one_sequence, (queries, fresh_key_heads, fresh_value_heads, cached_keys, value_cache_rows, lengths))
    slots = owners.shape[0]
    pieces = jnp.take(sectioned_rows, owners, axis=0)
    weight = pieces.reshape(slots, N_TENSOR, -1, D).transpose(1, 0, 2, 3).reshape(QUERY_HEADS * HEAD_SIZE, D)
    stream = residual.astype(jnp.float32) + jnp.dot(attended, weight, preferred_element_type=jnp.float32)
    inverse_rms = lax.rsqrt(lax.optimization_barrier(jnp.mean(stream * stream, axis=1, keepdims=True)) + 1e-06)
    normed = (stream * inverse_rms * norm_gain.astype(jnp.float32)[None, :]).astype(jnp.bfloat16)
    return (stream.astype(jnp.bfloat16), normed)
```

```python
import functools

import jax
import jax.numpy as jnp
from jax import lax
from jax.experimental import pallas as pl
from jax.experimental.pallas import tpu as pltpu
from jax.sharding import PartitionSpec as P

D = 5120
HEAD_SIZE = 128
HEADS = 8
SEQS = 4
SPAN = 4096
BATCH = 32
TENSOR = 8
GROUP = 8
CLANS = BATCH // GROUP
PIECE = 32
SLICE = D // TENSOR
FOLD = 384
REST = SLICE - FOLD
MESH = pl.DeviceIdType.MESH


def place_of(batch):
    y_lo, z, core = batch // 16, (batch // 2) % 8, batch % 2
    return (z // 2) * 8 + y_lo * 4 + (z % 2) * 2 + core


def batch_of(place):
    clan, y_lo, z_lo, core = place // 8, (place // 4) % 2, (place // 2) % 2, place % 2
    return y_lo * 16 + (clan * 2 + z_lo) * 2 + core


def slice_of(member, tensor):
    y_lo, z_lo, core = member // 4, (member // 2) % 2, member % 2
    x, y_hi = tensor // 2, tensor % 2
    return ((x + 2 * core + (y_lo + z_lo) % 2) % 4) * 2 + (y_hi + z_lo) % 2


def member_of(part, tensor):
    x, y_hi = tensor // 2, tensor % 2
    step = (part // 2 - x + 4) % 4
    z_lo = (part % 2 - y_hi + 2) % 2
    y_lo = (step % 2 + z_lo) % 2
    return y_lo * 4 + z_lo * 2 + step // 2


def kernel(
    q_ref,
    fresh_k_ref,
    fresh_v_ref,
    keys_hbm,
    values_hbm,
    lengths_ref,
    residual_ref,
    rows_hbm,
    owners_ref,
    gain_ref,
    stream_ref,
    normed_ref,
    keys,
    values,
    q_by_head,
    weights,
    attended,
    message,
    gathered,
    rows,
    partial,
    partials,
    square,
    squares,
    key_sem,
    value_sem,
    rows_send,
    rows_recv,
    att_send,
    att_recv,
    part_send,
    part_recv,
    sq_send,
    sq_recv,
):
    batch, tensor = lax.axis_index("batch"), lax.axis_index("tensor")
    place = place_of(batch)
    clan, member = place // GROUP, place % GROUP
    part = slice_of(member, tensor)
    mine = part == tensor

    for s in range(SEQS):
        pltpu.make_async_copy(keys_hbm.at[s, 0], keys.at[s], key_sem.at[s]).start()
    for s in range(SEQS):
        pltpu.make_async_copy(values_hbm.at[s, 0], values.at[s], value_sem.at[s]).start()

    barrier = pltpu.get_barrier_semaphore()

    def greet_batch(step, carry):
        pl.semaphore_signal(
            barrier, inc=1, device_id=((batch + step) % BATCH, tensor), device_id_type=MESH
        )
        return carry

    def greet_tensor(step, carry):
        pl.semaphore_signal(
            barrier, inc=1, device_id=(batch, (tensor + step) % TENSOR), device_id_type=MESH
        )
        return carry

    def greet_sources(step, carry):
        source = (tensor * CLANS + clan + step) % BATCH
        t = source // CLANS
        b = batch_of((source % CLANS) * GROUP + member_of(tensor, t))

        @pl.when(jnp.logical_not((b == batch) & (t == tensor)))
        def _():
            pl.semaphore_signal(barrier, inc=1, device_id=(b, t), device_id_type=MESH)

        return carry

    lax.fori_loop(1, BATCH, greet_batch, 0)
    lax.fori_loop(1, TENSOR, greet_tensor, 0)
    lax.fori_loop(0, BATCH, greet_sources, 0)
    pl.semaphore_wait(barrier, BATCH - 1 + TENSOR - 1 + BATCH - jnp.where(mine, 1, 0))

    def send_rows(step, carry):
        other = (member + step) % GROUP
        pltpu.make_async_remote_copy(
            src_ref=rows_hbm.at[0, :, pl.ds(pl.multiple_of(slice_of(other, tensor) * SLICE, 128), SLICE)],
            dst_ref=rows.at[member],
            send_sem=rows_send,
            recv_sem=rows_recv,
            device_id=(batch_of(clan * GROUP + other), tensor),
            device_id_type=MESH,
        ).start()
        return carry

    lax.fori_loop(1, GROUP, send_rows, 0)
    pltpu.make_async_copy(
        rows_hbm.at[0, :, pl.ds(pl.multiple_of(part * SLICE, 128), SLICE)],
        rows.at[member],
        rows_recv,
    ).start()

    q_all = q_ref[...].astype(jnp.float32)
    for h in range(HEADS):
        q_by_head[pl.ds(h, SEQS, stride=HEADS), :] = q_all[:, h * HEAD_SIZE : (h + 1) * HEAD_SIZE]
    fresh_k = fresh_k_ref[...].astype(jnp.float32)
    fresh_v = fresh_v_ref[...].astype(jnp.float32)
    scale = HEAD_SIZE ** (-0.5)
    position = lax.broadcasted_iota(jnp.int32, (HEADS, SPAN), 1)
    own_weights, totals = [], []
    for s in range(SEQS):
        pltpu.make_async_copy(keys_hbm.at[s, 0], keys.at[s], key_sem.at[s]).wait()
        q = q_by_head[s * HEADS : (s + 1) * HEADS, :]
        scores = (
            lax.dot_general(
                q.astype(jnp.bfloat16),
                keys[s],
                (((1,), (1,)), ((), ())),
                preferred_element_type=jnp.float32,
            )
            * scale
        )
        scores = jnp.where(position < lengths_ref[s], scores, -1e30)
        own = jnp.sum(q * fresh_k[s : s + 1, :], axis=1, keepdims=True) * scale
        top = jnp.maximum(jnp.max(scores, axis=1, keepdims=True), own)
        prob = jnp.exp(scores - top)
        own_prob = jnp.exp(own - top)
        totals.append(jnp.sum(prob, axis=1, keepdims=True) + own_prob)
        own_weights.append(own_prob.astype(jnp.bfloat16).astype(jnp.float32))
        weights[s] = prob.astype(jnp.bfloat16)
    for s in range(SEQS):
        pltpu.make_async_copy(values_hbm.at[s, 0], values.at[s], value_sem.at[s]).wait()
        mixed = lax.dot_general(
            weights[s], values[s], (((1,), (0,)), ((), ())), preferred_element_type=jnp.float32
        )
        mixed = (mixed + own_weights[s] * fresh_v[s : s + 1, :]) / totals[s]
        attended[s * HEADS : (s + 1) * HEADS, :] = mixed
        attended[(s + SEQS) * HEADS : (s + SEQS + 1) * HEADS, :] = mixed

    row = lax.broadcasted_iota(jnp.int32, (8, 128), 0)
    lane = lax.broadcasted_iota(jnp.int32, (8, 128), 1)
    code = (row // SEQS) * 4 + lane // PIECE
    blocks = [jnp.zeros((8, 128), jnp.float32)] * CLANS
    for k in range(BATCH):
        if k % 4 == 0:
            head = attended[pl.ds(k // 4, 8, stride=HEADS), :]
        target = place_of(owners_ref[k])
        turned = pltpu.roll(head, (target % 4 + 4 - k % 4) % 4 * PIECE, 1)
        blocks = [
            jnp.where(code == target - c * GROUP, turned, blocks[c]) for c in range(CLANS)
        ]
    for c in range(CLANS):
        message[c] = blocks[c].astype(jnp.bfloat16)

    def send_attended(step, carry):
        other = (place + step) % BATCH
        pltpu.make_async_remote_copy(
            src_ref=message.at[other // GROUP],
            dst_ref=gathered.at[batch],
            send_sem=att_send,
            recv_sem=att_recv,
            device_id=(batch_of(other), tensor),
            device_id_type=MESH,
        ).start()
        return carry

    lax.fori_loop(1, BATCH, send_attended, 0)
    pltpu.make_async_copy(message.at[clan], gathered.at[batch], att_recv).start()

    pad = jnp.zeros((SEQS, FOLD - REST), jnp.float32)

    def fold(x):
        return jnp.concatenate(
            [x[:, :FOLD], jnp.concatenate([x[:, FOLD:], pad], axis=1)], axis=0
        )

    residual = fold(residual_ref[...].astype(jnp.float32))
    gain = fold(jnp.broadcast_to(gain_ref[...].astype(jnp.float32), (SEQS, SLICE)))
    row3 = lax.broadcasted_iota(jnp.int32, (8, FOLD), 0)
    lane3 = lax.broadcasted_iota(jnp.int32, (8, FOLD), 1)
    used = (row3 < SEQS) | (lane3 < REST)

    pltpu.make_async_copy(rows, rows, rows_recv).wait()
    pltpu.make_async_copy(gathered, gathered, att_recv).wait()

    first = gathered[...].astype(jnp.float32)
    swapped = pltpu.roll(first, SEQS, 1).reshape(BATCH * 8, 128).astype(jnp.bfloat16)
    first = first.reshape(BATCH * 8, 128).astype(jnp.bfloat16)
    table = rows[...].reshape(GROUP * PIECE, SLICE)
    low = jnp.dot(
        jnp.concatenate([first, swapped], axis=1), table[:, :FOLD], preferred_element_type=jnp.float32
    )
    high = jnp.dot(
        jnp.concatenate([swapped, first], axis=1), table[:, FOLD:], preferred_element_type=jnp.float32
    )
    upper = lax.broadcasted_iota(jnp.int32, (BATCH * 8, REST), 0) % 8 < SEQS
    partial[:, :, :REST] = (
        jnp.where(upper, low[:, :REST], high).reshape(BATCH, 8, REST).astype(jnp.bfloat16)
    )
    partial[:, :, REST:] = low[:, REST:].reshape(BATCH, 8, FOLD - REST).astype(jnp.bfloat16)

    def send_partial(step, carry):
        other = (batch + step) % BATCH
        local = mine & (step == 0)

        @pl.when(jnp.logical_not(local))
        def _():
            pltpu.make_async_remote_copy(
                src_ref=partial.at[other],
                dst_ref=partials.at[tensor * CLANS + clan],
                send_sem=part_send,
                recv_sem=part_recv,
                device_id=(other, part),
                device_id_type=MESH,
            ).start()

        @pl.when(local)
        def _():
            pltpu.make_async_copy(
                partial.at[other], partials.at[tensor * CLANS + clan], part_recv
            ).start()

        return carry

    lax.fori_loop(0, BATCH, send_partial, 0)
    pltpu.make_async_copy(partials, partials, part_recv).wait()
    total = jnp.sum(partials[...].astype(jnp.float32), axis=0)
    stream = jnp.where(used, residual + total, 0.0)

    squared = stream * stream
    squared = squared[:, :128] + squared[:, 128:256] + squared[:, 256:]
    squared = squared + pltpu.roll(squared, SEQS, 0)
    square[...] = jnp.broadcast_to(jnp.sum(squared, axis=1, keepdims=True), (8, 128))

    def send_square(step, carry):
        pltpu.make_async_remote_copy(
            src_ref=square,
            dst_ref=squares.at[step - 1],
            send_sem=sq_send,
            recv_sem=sq_recv,
            device_id=(batch, (tensor + step) % TENSOR),
            device_id_type=MESH,
        ).start()
        return carry

    lax.fori_loop(1, TENSOR, send_square, 0)

    def unfold(x):
        return jnp.concatenate([x[:SEQS, :], x[SEQS:, :REST]], axis=1)

    stream_ref[...] = unfold(stream).astype(jnp.bfloat16)
    scaled = stream * gain
    pltpu.make_async_copy(squares, squares, sq_recv).wait()
    mean = (square[...] + jnp.sum(squares[...], axis=0)) / D
    inverse = lax.rsqrt(mean + 1e-6)[:, :1]
    normed_ref[...] = unfold(scaled * inverse).astype(jnp.bfloat16)

    pltpu.make_async_copy(squares, squares, sq_send).wait()
    pltpu.make_async_copy(rows.at[: GROUP - 1], rows.at[: GROUP - 1], rows_send).wait()
    pltpu.make_async_copy(gathered.at[: BATCH - 1], gathered.at[: BATCH - 1], att_send).wait()
    pltpu.make_async_copy(partial.at[: BATCH - 1], partial.at[: BATCH - 1], part_send).wait()

    @pl.when(jnp.logical_not(mine))
    def _():
        pltpu.make_async_copy(partial.at[0], partial.at[0], part_send).wait()


def local(
    queries,
    fresh_key_heads,
    fresh_value_heads,
    cached_keys,
    value_cache_rows,
    lengths,
    residual,
    sectioned_rows,
    owners,
    norm_gain,
):
    vmem = pl.BlockSpec(memory_space=pltpu.VMEM)
    smem = pl.BlockSpec(memory_space=pltpu.SMEM)
    anywhere = pl.BlockSpec(memory_space=pl.ANY)
    block = jax.ShapeDtypeStruct((SEQS, SLICE), jnp.bfloat16)
    bf16, f32 = jnp.bfloat16, jnp.float32
    return pl.pallas_call(
        kernel,
        out_shape=(block, block),
        in_specs=[vmem, vmem, vmem, anywhere, anywhere, smem, vmem, anywhere, smem, vmem],
        out_specs=(vmem, vmem),
        scratch_shapes=[
            pltpu.VMEM((SEQS, SPAN, HEAD_SIZE), bf16),
            pltpu.VMEM((SEQS, SPAN, HEAD_SIZE), bf16),
            pltpu.VMEM((SEQS * HEADS, HEAD_SIZE), f32),
            pltpu.VMEM((SEQS, HEADS, SPAN), bf16),
            pltpu.VMEM((2 * SEQS * HEADS, HEAD_SIZE), f32),
            pltpu.VMEM((CLANS, 8, 128), bf16),
            pltpu.VMEM((BATCH, 8, 128), bf16),
            pltpu.VMEM((GROUP, PIECE, SLICE), bf16),
            pltpu.VMEM((BATCH, 8, FOLD), bf16),
            pltpu.VMEM((BATCH, 8, FOLD), bf16),
            pltpu.VMEM((8, 128), f32),
            pltpu.VMEM((TENSOR - 1, 8, 128), f32),
            pltpu.SemaphoreType.DMA((SEQS,)),
            pltpu.SemaphoreType.DMA((SEQS,)),
        ]
        + [pltpu.SemaphoreType.DMA] * 8,
        compiler_params=pltpu.CompilerParams(
            collective_id=0, has_side_effects=True, vmem_limit_bytes=56 * 1024 * 1024
        ),
    )(
        queries,
        fresh_key_heads,
        fresh_value_heads,
        cached_keys,
        value_cache_rows,
        lengths,
        residual,
        sectioned_rows,
        owners,
        norm_gain.reshape(1, -1),
    )


def solution(mesh):
    return jax.shard_map(
        local,
        mesh=mesh,
        in_specs=(
            P("batch", "tensor"),
            P("batch", "tensor"),
            P("batch", "tensor"),
            P("batch", "tensor", None, None),
            P("batch", "tensor", None, None),
            P("batch"),
            P("batch", "tensor"),
            P("batch", "tensor", None),
            P(),
            P("tensor"),
        ),
        out_specs=(P("batch", "tensor"), P("batch", "tensor")),
        check_vma=False,
    )
```

```python
import functools

import jax
import jax.numpy as jnp
from jax import lax
from jax.experimental import pallas as pl
from jax.experimental.pallas import tpu as pltpu
from jax.sharding import PartitionSpec as P

D = 5120
HEAD_SIZE = 128
HEADS = 8
SEQS = 4
SPAN = 4096
BATCH = 32
TENSOR = 8
GROUP = 8
CLANS = BATCH // GROUP
PIECE = 32
SLICE = D // TENSOR
FOLD = 384
REST = SLICE - FOLD
MESH = pl.DeviceIdType.MESH


def place_of(batch):
    y_lo, z, core = batch // 16, (batch // 2) % 8, batch % 2
    return (z // 2) * 8 + y_lo * 4 + (z % 2) * 2 + core


def batch_of(place):
    clan, y_lo, z_lo, core = place // 8, (place // 4) % 2, (place // 2) % 2, place % 2
    return y_lo * 16 + (clan * 2 + z_lo) * 2 + core


def slice_of(member, tensor):
    y_lo, z_lo, core = member // 4, (member // 2) % 2, member % 2
    x, y_hi = tensor // 2, tensor % 2
    return ((x + 2 * core + (y_lo + z_lo) % 2) % 4) * 2 + (y_hi + z_lo) % 2


def member_of(part, tensor):
    x, y_hi = tensor // 2, tensor % 2
    step = (part // 2 - x + 4) % 4
    z_lo = (part % 2 - y_hi + 2) % 2
    y_lo = (step % 2 + z_lo) % 2
    return y_lo * 4 + z_lo * 2 + step // 2


def batch_at(batch, step):
    y_lo, z, core = batch // 16, (batch // 2) % 8, batch % 2
    ring, rest = step // 4, step % 4
    away = 4 + (ring // 2 + ring % 2) * (1 - 2 * (ring % 2))
    return (
        (y_lo + 1 - rest // 2) % 2 * 16 + (z + away) % 8 * 2 + (core + 1 - rest % 2) % 2
    )


def tensor_at(tensor, step):
    x, y_hi = tensor // 2, tensor % 2
    ring = step // 2
    away = 2 + (ring // 2 + ring % 2) * (1 - 2 * (ring % 2))
    return (x + away) % 4 * 2 + (y_hi + 1 - step % 2) % 2


def kernel(
    q_hbm,
    fresh_k_hbm,
    fresh_v_hbm,
    keys_hbm,
    values_hbm,
    lengths_hbm,
    residual_hbm,
    rows_hbm,
    owners_hbm,
    out_ref,
    q_ref,
    fresh_k_ref,
    fresh_v_ref,
    lengths_ref,
    residual_ref,
    owners_ref,
    keys,
    values,
    q_by_head,
    weights,
    attended,
    message,
    gathered,
    rows,
    partial,
    partials,
    square,
    squares,
    small_sem,
    key_sem,
    value_sem,
    rows_send,
    rows_recv,
    att_send,
    att_recv,
    part_send,
    part_recv,
    sq_send,
    sq_recv,
):
    batch, tensor = lax.axis_index("batch"), lax.axis_index("tensor")
    place = place_of(batch)
    clan, member = place // GROUP, place % GROUP
    part = slice_of(member, tensor)
    mine = part == tensor

    barrier = pltpu.get_barrier_semaphore()

    def greet_batch(step, carry):
        pl.semaphore_signal(
            barrier, inc=1, device_id=(batch_at(batch, step), tensor), device_id_type=MESH
        )
        return carry

    def greet_tensor(step, carry):
        pl.semaphore_signal(
            barrier, inc=1, device_id=(batch, tensor_at(tensor, step)), device_id_type=MESH
        )
        return carry

    lax.fori_loop(0, BATCH - 1, greet_batch, 0)
    lax.fori_loop(0, TENSOR - 1, greet_tensor, 0)

    small = [
        pltpu.make_async_copy(source, target, small_sem.at[i])
        for i, (source, target) in enumerate(
            (
                (q_hbm, q_ref),
                (fresh_k_hbm, fresh_k_ref),
                (fresh_v_hbm, fresh_v_ref),
                (lengths_hbm, lengths_ref),
                (residual_hbm, residual_ref),
                (owners_hbm, owners_ref),
            )
        )
    ]
    for copy in small:
        copy.start()
    for s in range(SEQS):
        pltpu.make_async_copy(keys_hbm.at[s, 0], keys.at[s], key_sem.at[s]).start()
    for s in range(SEQS):
        pltpu.make_async_copy(values_hbm.at[s, 0], values.at[s], value_sem.at[s]).start()

    pl.semaphore_wait(barrier, BATCH - 1 + TENSOR - 1)

    def send_rows(step, carry):
        other = (member + step) % GROUP
        pltpu.make_async_remote_copy(
            src_ref=rows_hbm.at[0, :, pl.ds(pl.multiple_of(slice_of(other, tensor) * SLICE, 128), SLICE)],
            dst_ref=rows.at[member],
            send_sem=rows_send,
            recv_sem=rows_recv,
            device_id=(batch_of(clan * GROUP + other), tensor),
            device_id_type=MESH,
        ).start()
        return carry

    lax.fori_loop(1, GROUP, send_rows, 0)
    pltpu.make_async_copy(
        rows_hbm.at[0, :, pl.ds(pl.multiple_of(part * SLICE, 128), SLICE)],
        rows.at[member],
        rows_recv,
    ).start()

    for copy in small:
        copy.wait()
    q_all = q_ref[...].astype(jnp.float32)
    for h in range(HEADS):
        q_by_head[pl.ds(h, SEQS, stride=HEADS), :] = q_all[:, h * HEAD_SIZE : (h + 1) * HEAD_SIZE]
    fresh_k = fresh_k_ref[...].astype(jnp.float32)
    fresh_v = fresh_v_ref[...].astype(jnp.float32)
    scale = HEAD_SIZE ** (-0.5)
    position = lax.broadcasted_iota(jnp.int32, (HEADS, SPAN), 1)
    own_weights, totals = [], []
    for s in range(SEQS):
        pltpu.make_async_copy(keys_hbm.at[s, 0], keys.at[s], key_sem.at[s]).wait()
        q = q_by_head[s * HEADS : (s + 1) * HEADS, :]
        scores = (
            lax.dot_general(
                q.astype(jnp.bfloat16),
                keys[s],
                (((1,), (1,)), ((), ())),
                preferred_element_type=jnp.float32,
            )
            * scale
        )
        scores = jnp.where(position < lengths_ref[s], scores, -1e30)
        own = jnp.sum(q * fresh_k[s : s + 1, :], axis=1, keepdims=True) * scale
        top = jnp.maximum(jnp.max(scores, axis=1, keepdims=True), own)
        prob = jnp.exp(scores - top)
        own_prob = jnp.exp(own - top)
        totals.append(jnp.sum(prob, axis=1, keepdims=True) + own_prob)
        own_weights.append(own_prob.astype(jnp.bfloat16).astype(jnp.float32))
        weights[s] = prob.astype(jnp.bfloat16)
    for s in range(SEQS):
        pltpu.make_async_copy(values_hbm.at[s, 0], values.at[s], value_sem.at[s]).wait()
        mixed = lax.dot_general(
            weights[s], values[s], (((1,), (0,)), ((), ())), preferred_element_type=jnp.float32
        )
        mixed = (mixed + own_weights[s] * fresh_v[s : s + 1, :]) / totals[s]
        attended[s * HEADS : (s + 1) * HEADS, :] = mixed
        attended[(s + SEQS) * HEADS : (s + SEQS + 1) * HEADS, :] = mixed

    row = lax.broadcasted_iota(jnp.int32, (8, 128), 0)
    lane = lax.broadcasted_iota(jnp.int32, (8, 128), 1)
    code = (row // SEQS) * 4 + lane // PIECE
    blocks = [jnp.zeros((8, 128), jnp.float32)] * CLANS
    for k in range(BATCH):
        if k % 4 == 0:
            head = attended[pl.ds(k // 4, 8, stride=HEADS), :]
        target = place_of(owners_ref[k])
        turned = pltpu.roll(head, (target % 4 + 4 - k % 4) % 4 * PIECE, 1)
        blocks = [
            jnp.where(code == target - c * GROUP, turned, blocks[c]) for c in range(CLANS)
        ]
    for c in range(CLANS):
        message[c] = blocks[c].astype(jnp.bfloat16)

    def send_attended(step, carry):
        other = batch_at(batch, step)
        pltpu.make_async_remote_copy(
            src_ref=message.at[place_of(other) // GROUP],
            dst_ref=gathered.at[batch],
            send_sem=att_send,
            recv_sem=att_recv,
            device_id=(other, tensor),
            device_id_type=MESH,
        ).start()
        return carry

    lax.fori_loop(0, BATCH - 1, send_attended, 0)
    pltpu.make_async_copy(message.at[clan], gathered.at[batch], att_recv).start()

    pad = jnp.zeros((SEQS, FOLD - REST), jnp.float32)

    def fold(x):
        return jnp.concatenate(
            [x[:, :FOLD], jnp.concatenate([x[:, FOLD:], pad], axis=1)], axis=0
        )

    residual = fold(residual_ref[...].astype(jnp.float32))
    row3 = lax.broadcasted_iota(jnp.int32, (8, FOLD), 0)
    lane3 = lax.broadcasted_iota(jnp.int32, (8, FOLD), 1)
    used = (row3 < SEQS) | (lane3 < REST)

    pltpu.make_async_copy(rows, rows, rows_recv).wait()
    pltpu.make_async_copy(gathered, gathered, att_recv).wait()

    first = gathered[...].astype(jnp.float32)
    swapped = pltpu.roll(first, SEQS, 1).reshape(BATCH * 8, 128).astype(jnp.bfloat16)
    first = first.reshape(BATCH * 8, 128).astype(jnp.bfloat16)
    table = rows[...].reshape(GROUP * PIECE, SLICE)
    low = jnp.dot(
        jnp.concatenate([first, swapped], axis=1), table[:, :FOLD], preferred_element_type=jnp.float32
    )
    high = jnp.dot(
        jnp.concatenate([swapped, first], axis=1), table[:, FOLD:], preferred_element_type=jnp.float32
    )
    upper = lax.broadcasted_iota(jnp.int32, (BATCH * 8, REST), 0) % 8 < SEQS
    partial[:, :, :REST] = (
        jnp.where(upper, low[:, :REST], high).reshape(BATCH, 8, REST).astype(jnp.bfloat16)
    )
    partial[:, :, REST:] = low[:, REST:].reshape(BATCH, 8, FOLD - REST).astype(jnp.bfloat16)

    def send_partial(step, carry):
        other = batch_at(batch, step)
        local = mine & (step == BATCH - 1)

        @pl.when(jnp.logical_not(local))
        def _():
            pltpu.make_async_remote_copy(
                src_ref=partial.at[other],
                dst_ref=partials.at[tensor * CLANS + clan],
                send_sem=part_send,
                recv_sem=part_recv,
                device_id=(other, part),
                device_id_type=MESH,
            ).start()

        @pl.when(local)
        def _():
            pltpu.make_async_copy(
                partial.at[other], partials.at[tensor * CLANS + clan], part_recv
            ).start()

        return carry

    lax.fori_loop(0, BATCH, send_partial, 0)
    pltpu.make_async_copy(partials, partials, part_recv).wait()
    total = jnp.sum(partials[...].astype(jnp.float32), axis=0)
    stream = jnp.where(used, residual + total, 0.0)

    squared = stream * stream
    squared = squared[:, :128] + squared[:, 128:256] + squared[:, 256:]
    squared = squared + pltpu.roll(squared, SEQS, 0)
    square[...] = jnp.broadcast_to(jnp.sum(squared, axis=1, keepdims=True), (8, 128))

    def send_square(step, carry):
        pltpu.make_async_remote_copy(
            src_ref=square,
            dst_ref=squares.at[step],
            send_sem=sq_send,
            recv_sem=sq_recv,
            device_id=(batch, tensor_at(tensor, step)),
            device_id_type=MESH,
        ).start()
        return carry

    lax.fori_loop(0, TENSOR - 1, send_square, 0)

    def unfold(x):
        return jnp.concatenate([x[:SEQS, :], x[SEQS:, :REST]], axis=1)

    out_ref[0] = unfold(stream)
    pltpu.make_async_copy(squares, squares, sq_recv).wait()
    mean = (square[...] + jnp.sum(squares[...], axis=0)) / D
    inverse = lax.rsqrt(mean + 1e-6)[:, :1]
    out_ref[1] = unfold(stream * inverse)

    pltpu.make_async_copy(squares, squares, sq_send).wait()
    pltpu.make_async_copy(rows.at[: GROUP - 1], rows.at[: GROUP - 1], rows_send).wait()
    pltpu.make_async_copy(gathered.at[: BATCH - 1], gathered.at[: BATCH - 1], att_send).wait()
    pltpu.make_async_copy(partial.at[: BATCH - 1], partial.at[: BATCH - 1], part_send).wait()

    @pl.when(jnp.logical_not(mine))
    def _():
        pltpu.make_async_copy(partial.at[0], partial.at[0], part_send).wait()


def local(
    queries,
    fresh_key_heads,
    fresh_value_heads,
    cached_keys,
    value_cache_rows,
    lengths,
    residual,
    sectioned_rows,
    owners,
    norm_gain,
):
    anywhere = pl.BlockSpec(memory_space=pl.ANY)
    bf16, f32 = jnp.bfloat16, jnp.float32
    out = pl.pallas_call(
        kernel,
        out_shape=jax.ShapeDtypeStruct((2, SEQS, SLICE), f32),
        in_specs=[anywhere] * 9,
        out_specs=pl.BlockSpec(memory_space=pltpu.VMEM),
        scratch_shapes=[
            pltpu.VMEM((SEQS, HEADS * HEAD_SIZE), bf16),
            pltpu.VMEM((SEQS, HEAD_SIZE), bf16),
            pltpu.VMEM((SEQS, HEAD_SIZE), bf16),
            pltpu.SMEM((SEQS,), jnp.int32),
            pltpu.VMEM((SEQS, SLICE), bf16),
            pltpu.SMEM((BATCH,), jnp.int32),
            pltpu.VMEM((SEQS, SPAN, HEAD_SIZE), bf16),
            pltpu.VMEM((SEQS, SPAN, HEAD_SIZE), bf16),
            pltpu.VMEM((SEQS * HEADS, HEAD_SIZE), f32),
            pltpu.VMEM((SEQS, HEADS, SPAN), bf16),
            pltpu.VMEM((2 * SEQS * HEADS, HEAD_SIZE), f32),
            pltpu.VMEM((CLANS, 8, 128), bf16),
            pltpu.VMEM((BATCH, 8, 128), bf16),
            pltpu.VMEM((GROUP, PIECE, SLICE), bf16),
            pltpu.VMEM((BATCH, 8, FOLD), bf16),
            pltpu.VMEM((BATCH, 8, FOLD), bf16),
            pltpu.VMEM((8, 128), f32),
            pltpu.VMEM((TENSOR - 1, 8, 128), f32),
            pltpu.SemaphoreType.DMA((6,)),
            pltpu.SemaphoreType.DMA((SEQS,)),
            pltpu.SemaphoreType.DMA((SEQS,)),
        ]
        + [pltpu.SemaphoreType.DMA] * 8,
        compiler_params=pltpu.CompilerParams(
            collective_id=0, has_side_effects=True, vmem_limit_bytes=56 * 1024 * 1024
        ),
    )(
        queries,
        fresh_key_heads,
        fresh_value_heads,
        cached_keys,
        value_cache_rows,
        lengths,
        residual,
        sectioned_rows,
        owners,
    )
    return out[0].astype(bf16), (out[1] * norm_gain.astype(f32)).astype(bf16)


def solution(mesh):
    return jax.shard_map(
        local,
        mesh=mesh,
        in_specs=(
            P("batch", "tensor"),
            P("batch", "tensor"),
            P("batch", "tensor"),
            P("batch", "tensor", None, None),
            P("batch", "tensor", None, None),
            P("batch"),
            P("batch", "tensor"),
            P("batch", "tensor", None),
            P(),
            P("tensor"),
        ),
        out_specs=(P("batch", "tensor"), P("batch", "tensor")),
        check_vma=False,
    )
```

```python
import functools

import jax
import jax.numpy as jnp
from jax import lax
from jax.experimental import pallas as pl
from jax.experimental.pallas import tpu as pltpu
from jax.sharding import PartitionSpec as P

D = 5120
HEAD_SIZE = 128
HEADS = 8
SEQS = 4
SPAN = 4096
BATCH = 32
TENSOR = 8
GROUP = 8
CLANS = BATCH // GROUP
PIECE = 32
SLICE = D // TENSOR
MESH = pl.DeviceIdType.MESH


def place_of(batch):
    return ((batch >> 2 & 3) << 3) + ((batch >> 4) << 2) + (batch & 3)


def batch_of(place):
    return ((place >> 2 & 1) << 4) + ((place >> 3) << 2) + (place & 3)


def slice_of(member, tensor):
    step = 2 * (member & 1) + ((member >> 2) ^ (member >> 1 & 1))
    return ((tensor + 2 * step) & 7) ^ (member >> 1 & 1)


def batch_at(batch, step):
    ring, rest = step >> 2, 3 - (step & 3)
    away = 4 + ((ring + 1) >> 1) * (1 - 2 * (ring & 1))
    return ((batch & 16) ^ ((rest & 2) << 3)) + ((((batch & 15) + 2 * away) & 15) ^ (rest & 1))


def tensor_at(tensor, step):
    ring = step >> 1
    away = 2 + ((ring + 1) >> 1) * (1 - 2 * (ring & 1))
    return ((tensor + 2 * away) & 7) ^ (1 - (step & 1))


def kernel(
    q_hbm,
    fresh_k_hbm,
    fresh_v_hbm,
    keys_hbm,
    values_hbm,
    lengths_hbm,
    residual_hbm,
    rows_hbm,
    owners_hbm,
    out_ref,
    q_ref,
    fresh_k_ref,
    fresh_v_ref,
    lengths_ref,
    residual_ref,
    owners_ref,
    keys,
    values,
    q_by_head,
    weights,
    attended,
    goals,
    message,
    gathered,
    rows,
    partial,
    partials,
    square,
    squares,
    small_sem,
    key_sem,
    value_sem,
    rows_send,
    rows_recv,
    att_send,
    att_recv,
    part_send,
    part_recv,
    sq_send,
    sq_recv,
):
    batch, tensor = lax.axis_index("batch"), lax.axis_index("tensor")
    place = place_of(batch)
    clan, member = place >> 3, place & 7
    part = slice_of(member, tensor)
    mine = part == tensor

    small = [
        pltpu.make_async_copy(source, target, small_sem.at[i])
        for i, (source, target) in enumerate(
            (
                (q_hbm, q_ref),
                (fresh_k_hbm, fresh_k_ref),
                (fresh_v_hbm, fresh_v_ref),
                (lengths_hbm, lengths_ref),
                (residual_hbm, residual_ref),
                (owners_hbm, owners_ref),
            )
        )
    ]
    for copy in small:
        copy.start()
    for s in range(SEQS):
        pltpu.make_async_copy(keys_hbm.at[s, 0], keys.at[s], key_sem.at[s]).start()
    for s in range(SEQS):
        pltpu.make_async_copy(values_hbm.at[s, 0], values.at[s], value_sem.at[s]).start()


    barrier = pltpu.get_barrier_semaphore()

    def greet_batch(step, carry):
        pl.semaphore_signal(
            barrier, inc=1, device_id=(batch_at(batch, step), tensor), device_id_type=MESH
        )
        return carry

    def greet_tensor(step, carry):
        pl.semaphore_signal(
            barrier, inc=1, device_id=(batch, tensor_at(tensor, step)), device_id_type=MESH
        )
        return carry

    lax.fori_loop(0, 4, greet_batch, 0)
    lax.fori_loop(0, TENSOR - 1, greet_tensor, 0)
    lax.fori_loop(4, BATCH - 1, greet_batch, 0)

    for copy in small:
        copy.wait()

    row = lax.broadcasted_iota(jnp.int32, (8, 128), 0)
    lane = lax.broadcasted_iota(jnp.int32, (8, 128), 1)
    block = lane // PIECE
    code = (row // SEQS) * 4 + block
    for h in range(HEADS):
        targets = [place_of(owners_ref[4 * h + j]) for j in range(4)]
        for r in range(4):
            goal = jnp.full((8, 128), targets[(3 - r) % 4], jnp.int32)
            for j in range(3):
                goal = jnp.where(block == j, targets[(j - r) % 4], goal)
            goals[h * 4 + r] = goal - code

    q_all = q_ref[...].astype(jnp.float32)
    for h in range(HEADS):
        q_by_head[pl.ds(h, SEQS, stride=HEADS), :] = q_all[:, h * HEAD_SIZE : (h + 1) * HEAD_SIZE]
    fresh_k = fresh_k_ref[...].astype(jnp.float32)
    fresh_v = fresh_v_ref[...].astype(jnp.float32)
    scale = HEAD_SIZE ** (-0.5)
    position = lax.broadcasted_iota(jnp.int32, (HEADS, SPAN), 1)
    for s in range(SEQS):
        pltpu.make_async_copy(keys_hbm.at[s, 0], keys.at[s], key_sem.at[s]).wait()
    own_weights, totals = [], []
    for s in range(SEQS):
        q = q_by_head[s * HEADS : (s + 1) * HEADS, :]
        scores = (
            lax.dot_general(
                q.astype(jnp.bfloat16),
                keys[s],
                (((1,), (1,)), ((), ())),
                preferred_element_type=jnp.float32,
            )
            * scale
        )
        scores = jnp.where(position < lengths_ref[s], scores, -1e30)
        own = jnp.sum(q * fresh_k[s : s + 1, :], axis=1, keepdims=True) * scale
        top = jnp.maximum(jnp.max(scores, axis=1, keepdims=True), own)
        prob = jnp.exp(scores - top)
        own_prob = jnp.exp(own - top)
        totals.append(jnp.sum(prob, axis=1, keepdims=True) + own_prob)
        own_weights.append(own_prob.astype(jnp.bfloat16).astype(jnp.float32))
        weights[s] = prob.astype(jnp.bfloat16)

    pl.semaphore_wait(barrier, BATCH - 1 + TENSOR - 1)

    def send_rows(step, carry):
        other = (member + step) & 7
        pltpu.make_async_remote_copy(
            src_ref=rows_hbm.at[0, :, pl.ds(pl.multiple_of(slice_of(other, tensor) * SLICE, 128), SLICE)],
            dst_ref=rows.at[member],
            send_sem=rows_send,
            recv_sem=rows_recv,
            device_id=(batch_of(clan * GROUP + other), tensor),
            device_id_type=MESH,
        ).start()
        return carry

    lax.fori_loop(1, GROUP, send_rows, 0)
    pltpu.make_async_copy(
        rows_hbm.at[0, :, pl.ds(pl.multiple_of(part * SLICE, 128), SLICE)],
        rows.at[member],
        rows_recv,
    ).start()

    for s in range(SEQS):
        pltpu.make_async_copy(values_hbm.at[s, 0], values.at[s], value_sem.at[s]).wait()
    for s in range(SEQS):
        mixed = lax.dot_general(
            weights[s], values[s], (((1,), (0,)), ((), ())), preferred_element_type=jnp.float32
        )
        mixed = (mixed + own_weights[s] * fresh_v[s : s + 1, :]) / totals[s]
        attended[s * HEADS : (s + 1) * HEADS, :] = mixed
        attended[(s + SEQS) * HEADS : (s + SEQS + 1) * HEADS, :] = mixed

    blocks = [jnp.zeros((8, 128), jnp.float32)] * CLANS
    for h in range(HEADS):
        head = attended[pl.ds(h, 8, stride=HEADS), :]
        for r in range(4):
            turned = pltpu.roll(head, r * PIECE, 1) if r else head
            goal = goals[h * 4 + r]
            blocks = [jnp.where(goal == c * GROUP, turned, blocks[c]) for c in range(CLANS)]
    for c in range(CLANS):
        message[c] = blocks[c].astype(jnp.bfloat16)

    def send_attended(step, carry):
        other = batch_at(batch, step)
        pltpu.make_async_remote_copy(
            src_ref=message.at[place_of(other) >> 3],
            dst_ref=gathered.at[batch],
            send_sem=att_send,
            recv_sem=att_recv,
            device_id=(other, tensor),
            device_id_type=MESH,
        ).start()
        return carry

    lax.fori_loop(0, BATCH - 1, send_attended, 0)
    pltpu.make_async_copy(message.at[clan], gathered.at[batch], att_recv).start()

    pltpu.make_async_copy(rows, rows, rows_recv).wait()
    pltpu.make_async_copy(gathered, gathered, att_recv).wait()

    first = gathered[...].astype(jnp.float32)
    swapped = pltpu.roll(first, SEQS, 1).reshape(BATCH * 8, 128).astype(jnp.bfloat16)
    first = first.reshape(BATCH * 8, 128).astype(jnp.bfloat16)
    table = rows[...].reshape(GROUP * PIECE, SLICE)
    product = jnp.dot(
        jnp.concatenate([first, swapped], axis=1), table, preferred_element_type=jnp.float32
    )
    partial[...] = product.reshape(BATCH, 8, SLICE)[:, :SEQS].astype(jnp.bfloat16)

    def send_partial(step, carry):
        other = batch_at(batch, step)
        local = mine & (step == BATCH - 1)

        @pl.when(jnp.logical_not(local))
        def _():
            pltpu.make_async_remote_copy(
                src_ref=partial.at[other],
                dst_ref=partials.at[tensor * CLANS + clan],
                send_sem=part_send,
                recv_sem=part_recv,
                device_id=(other, part),
                device_id_type=MESH,
            ).start()

        @pl.when(local)
        def _():
            pltpu.make_async_copy(
                partial.at[other], partials.at[tensor * CLANS + clan], part_recv
            ).start()

        return carry

    lax.fori_loop(0, BATCH, send_partial, 0)
    pltpu.make_async_copy(partials, partials, part_recv).wait()
    total = jnp.sum(partials[...].astype(jnp.float32), axis=0)
    stream = residual_ref[...].astype(jnp.float32) + total

    squared = jnp.sum(stream * stream, axis=1, keepdims=True)
    square[...] = jnp.broadcast_to(squared, (SEQS, 128))

    def send_square(step, carry):
        pltpu.make_async_remote_copy(
            src_ref=square,
            dst_ref=squares.at[step],
            send_sem=sq_send,
            recv_sem=sq_recv,
            device_id=(batch, tensor_at(tensor, step)),
            device_id_type=MESH,
        ).start()
        return carry

    lax.fori_loop(0, TENSOR - 1, send_square, 0)

    out_ref[0] = stream
    pltpu.make_async_copy(squares, squares, sq_recv).wait()
    mean = (squared + jnp.sum(squares[...], axis=0)[:, :1]) / D
    inverse = lax.rsqrt(mean + 1e-6)
    out_ref[1] = stream * inverse

    pltpu.make_async_copy(squares, squares, sq_send).wait()
    pltpu.make_async_copy(rows.at[: GROUP - 1], rows.at[: GROUP - 1], rows_send).wait()
    pltpu.make_async_copy(gathered.at[: BATCH - 1], gathered.at[: BATCH - 1], att_send).wait()
    pltpu.make_async_copy(partial.at[: BATCH - 1], partial.at[: BATCH - 1], part_send).wait()

    @pl.when(jnp.logical_not(mine))
    def _():
        pltpu.make_async_copy(partial.at[0], partial.at[0], part_send).wait()


def finish(x_ref, gain_ref, stream_ref, normed_ref):
    stream_ref[...] = x_ref[0].astype(jnp.bfloat16)
    gain = gain_ref[...].astype(jnp.float32).reshape(1, SLICE)
    normed_ref[...] = (x_ref[1] * gain).astype(jnp.bfloat16)


def local(
    queries,
    fresh_key_heads,
    fresh_value_heads,
    cached_keys,
    value_cache_rows,
    lengths,
    residual,
    sectioned_rows,
    owners,
    norm_gain,
):
    anywhere = pl.BlockSpec(memory_space=pl.ANY)
    bf16, f32 = jnp.bfloat16, jnp.float32
    out = pl.pallas_call(
        kernel,
        out_shape=pltpu.VMEM((2, SEQS, SLICE), f32),
        in_specs=[anywhere] * 9,
        out_specs=pl.BlockSpec(memory_space=pltpu.VMEM),
        scratch_shapes=[
            pltpu.VMEM((SEQS, HEADS * HEAD_SIZE), bf16),
            pltpu.VMEM((SEQS, HEAD_SIZE), bf16),
            pltpu.VMEM((SEQS, HEAD_SIZE), bf16),
            pltpu.SMEM((SEQS,), jnp.int32),
            pltpu.VMEM((SEQS, SLICE), bf16),
            pltpu.SMEM((BATCH,), jnp.int32),
            pltpu.VMEM((SEQS, SPAN, HEAD_SIZE), bf16),
            pltpu.VMEM((SEQS, SPAN, HEAD_SIZE), bf16),
            pltpu.VMEM((SEQS * HEADS, HEAD_SIZE), f32),
            pltpu.VMEM((SEQS, HEADS, SPAN), bf16),
            pltpu.VMEM((2 * SEQS * HEADS, HEAD_SIZE), f32),
            pltpu.VMEM((HEADS * 4, 8, 128), jnp.int32),
            pltpu.VMEM((CLANS, 8, 128), bf16),
            pltpu.VMEM((BATCH, 8, 128), bf16),
            pltpu.VMEM((GROUP, PIECE, SLICE), bf16),
            pltpu.VMEM((BATCH, SEQS, SLICE), bf16),
            pltpu.VMEM((BATCH, SEQS, SLICE), bf16),
            pltpu.VMEM((SEQS, 128), f32),
            pltpu.VMEM((TENSOR - 1, SEQS, 128), f32),
            pltpu.SemaphoreType.DMA((6,)),
            pltpu.SemaphoreType.DMA((SEQS,)),
            pltpu.SemaphoreType.DMA((SEQS,)),
        ]
        + [pltpu.SemaphoreType.DMA] * 8,
        compiler_params=pltpu.CompilerParams(
            collective_id=0, has_side_effects=True, vmem_limit_bytes=56 * 1024 * 1024
        ),
    )(
        queries,
        fresh_key_heads,
        fresh_value_heads,
        cached_keys,
        value_cache_rows,
        lengths,
        residual,
        sectioned_rows,
        owners,
    )
    block = jax.ShapeDtypeStruct((SEQS, SLICE), bf16)
    out = pltpu.with_memory_space_constraint(out, pltpu.VMEM)
    return pl.pallas_call(finish, out_shape=(block, block))(out, norm_gain)


def solution(mesh):
    return jax.shard_map(
        local,
        mesh=mesh,
        in_specs=(
            P("batch", "tensor"),
            P("batch", "tensor"),
            P("batch", "tensor"),
            P("batch", "tensor", None, None),
            P("batch", "tensor", None, None),
            P("batch"),
            P("batch", "tensor"),
            P("batch", "tensor", None),
            P(),
            P("tensor"),
        ),
        out_specs=(P("batch", "tensor"), P("batch", "tensor")),
        check_vma=False,
    )
```

```python
import functools

import jax
import jax.numpy as jnp
from jax import lax
from jax.experimental import pallas as pl
from jax.experimental.pallas import tpu as pltpu
from jax.sharding import PartitionSpec as P

D = 5120
HEAD_SIZE = 128
HEADS = 8
SEQS = 4
SPAN = 4096
BATCH = 32
TENSOR = 8
GROUP = 8
CLANS = BATCH // GROUP
PART = BATCH // 4
PIECE = 32
SLICE = D // TENSOR
MESH = pl.DeviceIdType.MESH


def place_of(batch):
    return ((batch >> 2 & 3) << 3) + ((batch >> 4) << 2) + (batch & 3)


def batch_of(place):
    return ((place >> 2 & 1) << 4) + ((place >> 3) << 2) + (place & 3)


def slice_of(member, tensor):
    step = 2 * (member & 1) + ((member >> 2) ^ (member >> 1 & 1))
    return ((tensor + 2 * step) & 7) ^ (member >> 1 & 1)


def batch_at(batch, step):
    ring, rest = step >> 2, 3 - (step & 3)
    away = 4 + ((ring + 1) >> 1) * (1 - 2 * (ring & 1))
    return ((batch & 16) ^ ((rest & 2) << 3)) + ((((batch & 15) + 2 * away) & 15) ^ (rest & 1))


def tensor_at(tensor, step):
    ring = step >> 1
    away = 2 + ((ring + 1) >> 1) * (1 - 2 * (ring & 1))
    return ((tensor + 2 * away) & 7) ^ (1 - (step & 1))


def slot_of(batch):
    return ((batch & 14) << 1) + ((batch >> 4) << 1) + (batch & 1)


def batch_of_slot(slot):
    return ((slot >> 1 & 1) << 4) + ((slot >> 2) << 1) + (slot & 1)


def kernel(
    q_hbm,
    fresh_k_hbm,
    fresh_v_hbm,
    keys_hbm,
    values_hbm,
    lengths_hbm,
    residual_hbm,
    rows_hbm,
    owners_hbm,
    out_ref,
    q_ref,
    fresh_k_ref,
    fresh_v_ref,
    lengths_ref,
    residual_ref,
    owners_ref,
    keys,
    values,
    q_by_head,
    weights,
    attended,
    goals,
    message,
    gathered,
    rows,
    partial,
    partials,
    square,
    squares,
    small_sem,
    key_sem,
    value_sem,
    rows_send,
    rows_recv,
    att_send,
    att_recv,
    part_send,
    part_recv,
    sq_send,
    sq_recv,
):
    batch, tensor = lax.axis_index("batch"), lax.axis_index("tensor")
    place = place_of(batch)
    clan, member = place >> 3, place & 7
    part = slice_of(member, tensor)
    mine = part == tensor
    late = (batch & 8) != 0

    small = [
        pltpu.make_async_copy(source, target, small_sem.at[i])
        for i, (source, target) in enumerate(
            (
                (q_hbm, q_ref),
                (fresh_k_hbm, fresh_k_ref),
                (fresh_v_hbm, fresh_v_ref),
                (lengths_hbm, lengths_ref),
                (residual_hbm, residual_ref),
                (owners_hbm, owners_ref),
            )
        )
    ]
    for copy in small:
        copy.start()
    for s in range(SEQS):
        pltpu.make_async_copy(keys_hbm.at[s, 0], keys.at[s], key_sem.at[s]).start()
    for s in range(SEQS):
        pltpu.make_async_copy(values_hbm.at[s, 0], values.at[s], value_sem.at[s]).start()


    barrier = pltpu.get_barrier_semaphore()

    def greet_batch(step, carry):
        pl.semaphore_signal(
            barrier, inc=1, device_id=(batch_at(batch, step), tensor), device_id_type=MESH
        )
        return carry

    def greet_tensor(step, carry):
        pl.semaphore_signal(
            barrier, inc=1, device_id=(batch, tensor_at(tensor, step)), device_id_type=MESH
        )
        return carry

    lax.fori_loop(0, 4, greet_batch, 0)
    lax.fori_loop(0, TENSOR - 1, greet_tensor, 0)
    lax.fori_loop(4, BATCH - 1, greet_batch, 0)

    def send_rows(step, carry):
        other = (member + step) & 7
        pltpu.make_async_remote_copy(
            src_ref=rows_hbm.at[0, :, pl.ds(pl.multiple_of(slice_of(other, tensor) * SLICE, 128), SLICE)],
            dst_ref=rows.at[member],
            send_sem=rows_send,
            recv_sem=rows_recv,
            device_id=(batch_of(clan * GROUP + other), tensor),
            device_id_type=MESH,
        ).start()
        return carry

    def open_up():
        pl.semaphore_wait(barrier, BATCH - 1 + TENSOR - 1)

    def recut():
        lax.fori_loop(1, GROUP, send_rows, 0)
        pltpu.make_async_copy(
            rows_hbm.at[0, :, pl.ds(pl.multiple_of(part * SLICE, 128), SLICE)],
            rows.at[member],
            rows_recv,
        ).start()


    for copy in small:
        copy.wait()

    row = lax.broadcasted_iota(jnp.int32, (8, 128), 0)
    lane = lax.broadcasted_iota(jnp.int32, (8, 128), 1)
    block = lane // PIECE
    code = (row // SEQS) * 4 + block
    for h in range(HEADS):
        targets = [place_of(owners_ref[4 * h + j]) for j in range(4)]
        for r in range(4):
            goal = jnp.full((8, 128), targets[(3 - r) % 4], jnp.int32)
            for j in range(3):
                goal = jnp.where(block == j, targets[(j - r) % 4], goal)
            goals[h * 4 + r] = goal - code

    q_all = q_ref[...].astype(jnp.float32)
    for h in range(HEADS):
        q_by_head[pl.ds(h, SEQS, stride=HEADS), :] = q_all[:, h * HEAD_SIZE : (h + 1) * HEAD_SIZE]
    fresh_k = fresh_k_ref[...].astype(jnp.float32)
    fresh_v = fresh_v_ref[...].astype(jnp.float32)
    scale = HEAD_SIZE ** (-0.5)
    position = lax.broadcasted_iota(jnp.int32, (HEADS, SPAN), 1)
    own_weights, totals = [], []
    for s in range(SEQS):
        if s == 2:
            @pl.when(late)
            def _():
                open_up()
                recut()

        if s % 2 == 0:
            for r in range(s, s + 2):
                pltpu.make_async_copy(keys_hbm.at[r, 0], keys.at[r], key_sem.at[r]).wait()
        q = q_by_head[s * HEADS : (s + 1) * HEADS, :]
        scores = (
            lax.dot_general(
                q.astype(jnp.bfloat16),
                keys[s],
                (((1,), (1,)), ((), ())),
                preferred_element_type=jnp.float32,
            )
            * scale
        )
        scores = jnp.where(position < lengths_ref[s], scores, -1e30)
        own = jnp.sum(q * fresh_k[s : s + 1, :], axis=1, keepdims=True) * scale
        top = jnp.maximum(jnp.max(scores, axis=1, keepdims=True), own)
        prob = jnp.exp(scores - top)
        own_prob = jnp.exp(own - top)
        totals.append(jnp.sum(prob, axis=1, keepdims=True) + own_prob)
        own_weights.append(own_prob.astype(jnp.bfloat16).astype(jnp.float32))
        weights[s] = prob.astype(jnp.bfloat16)

    for s in range(SEQS):
        pltpu.make_async_copy(values_hbm.at[s, 0], values.at[s], value_sem.at[s]).wait()
    for s in range(SEQS):
        mixed = lax.dot_general(
            weights[s], values[s], (((1,), (0,)), ((), ())), preferred_element_type=jnp.float32
        )
        mixed = (mixed + own_weights[s] * fresh_v[s : s + 1, :]) / totals[s]
        attended[s * HEADS : (s + 1) * HEADS, :] = mixed
        attended[(s + SEQS) * HEADS : (s + SEQS + 1) * HEADS, :] = mixed

    blocks = [jnp.zeros((8, 128), jnp.float32)] * CLANS
    for h in range(HEADS):
        head = attended[pl.ds(h, 8, stride=HEADS), :]
        for r in range(4):
            turned = pltpu.roll(head, r * PIECE, 1) if r else head
            goal = goals[h * 4 + r]
            blocks = [jnp.where(goal == c * GROUP, turned, blocks[c]) for c in range(CLANS)]
    for c in range(CLANS):
        message[c] = blocks[c].astype(jnp.bfloat16)

    slot = slot_of(batch)
    chunk = slot // PART

    def send_attended(step, carry):
        other = batch_at(batch, step)
        pltpu.make_async_remote_copy(
            src_ref=message.at[place_of(other) >> 3],
            dst_ref=gathered.at[slot],
            send_sem=att_send,
            recv_sem=att_recv.at[chunk],
            device_id=(other, tensor),
            device_id_type=MESH,
        ).start()
        return carry

    @pl.when(jnp.logical_not(late))
    def _():
        open_up()

    lax.fori_loop(0, BATCH - 1, send_attended, 0)
    pltpu.make_async_copy(message.at[clan], gathered.at[slot], att_recv.at[chunk]).start()

    @pl.when(jnp.logical_not(late))
    def _():
        recut()


    pltpu.make_async_copy(rows, rows, rows_recv).wait()


    def project(turn, carry):
        table = rows[...].reshape(GROUP * PIECE, SLICE)
        here = pl.ds(turn * PART, PART)
        pltpu.make_async_copy(gathered.at[here], gathered.at[here], att_recv.at[turn]).wait()
        first = gathered[here].astype(jnp.float32)
        swapped = pltpu.roll(first, SEQS, 1).reshape(PART * 8, 128).astype(jnp.bfloat16)
        first = first.reshape(PART * 8, 128).astype(jnp.bfloat16)
        product = jnp.dot(
            jnp.concatenate([first, swapped], axis=1), table, preferred_element_type=jnp.float32
        )
        partial[here] = product.reshape(PART, 8, SLICE)[:, :SEQS].astype(jnp.bfloat16)

        def send_partial(step, carry):
            other = turn * PART + step
            local = mine & (other == slot)

            @pl.when(jnp.logical_not(local))
            def _():
                pltpu.make_async_remote_copy(
                    src_ref=partial.at[other],
                    dst_ref=partials.at[tensor * CLANS + clan],
                    send_sem=part_send,
                    recv_sem=part_recv,
                    device_id=(batch_of_slot(other), part),
                    device_id_type=MESH,
                ).start()

            @pl.when(local)
            def _():
                pltpu.make_async_copy(
                    partial.at[other], partials.at[tensor * CLANS + clan], part_recv
                ).start()

            return carry

        lax.fori_loop(0, PART, send_partial, 0)
        return carry

    lax.fori_loop(0, BATCH // PART, project, 0)
    pltpu.make_async_copy(partials, partials, part_recv).wait()
    total = jnp.sum(partials[...].astype(jnp.float32), axis=0)
    stream = residual_ref[...].astype(jnp.float32) + total

    squared = jnp.sum(stream * stream, axis=1, keepdims=True)
    square[...] = jnp.broadcast_to(squared, (SEQS, 128))

    def send_square(step, carry):
        pltpu.make_async_remote_copy(
            src_ref=square,
            dst_ref=squares.at[step],
            send_sem=sq_send,
            recv_sem=sq_recv,
            device_id=(batch, tensor_at(tensor, step)),
            device_id_type=MESH,
        ).start()
        return carry

    lax.fori_loop(0, TENSOR - 1, send_square, 0)

    out_ref[0] = stream
    pltpu.make_async_copy(squares, squares, sq_recv).wait()
    mean = (squared + jnp.sum(squares[...], axis=0)[:, :1]) / D
    inverse = lax.rsqrt(mean + 1e-6)
    out_ref[1] = stream * inverse

    pltpu.make_async_copy(squares, squares, sq_send).wait()
    pltpu.make_async_copy(rows.at[: GROUP - 1], rows.at[: GROUP - 1], rows_send).wait()
    pltpu.make_async_copy(gathered.at[: BATCH - 1], gathered.at[: BATCH - 1], att_send).wait()
    pltpu.make_async_copy(partial.at[: BATCH - 1], partial.at[: BATCH - 1], part_send).wait()

    @pl.when(jnp.logical_not(mine))
    def _():
        pltpu.make_async_copy(partial.at[0], partial.at[0], part_send).wait()


def finish(x_ref, gain_ref, stream_ref, normed_ref):
    stream_ref[...] = x_ref[0].astype(jnp.bfloat16)
    gain = gain_ref[...].astype(jnp.float32).reshape(1, SLICE)
    normed_ref[...] = (x_ref[1] * gain).astype(jnp.bfloat16)


def local(
    queries,
    fresh_key_heads,
    fresh_value_heads,
    cached_keys,
    value_cache_rows,
    lengths,
    residual,
    sectioned_rows,
    owners,
    norm_gain,
):
    anywhere = pl.BlockSpec(memory_space=pl.ANY)
    bf16, f32 = jnp.bfloat16, jnp.float32
    out = pl.pallas_call(
        kernel,
        out_shape=pltpu.VMEM((2, SEQS, SLICE), f32),
        in_specs=[anywhere] * 9,
        out_specs=pl.BlockSpec(memory_space=pltpu.VMEM),
        scratch_shapes=[
            pltpu.VMEM((SEQS, HEADS * HEAD_SIZE), bf16),
            pltpu.VMEM((SEQS, HEAD_SIZE), bf16),
            pltpu.VMEM((SEQS, HEAD_SIZE), bf16),
            pltpu.SMEM((SEQS,), jnp.int32),
            pltpu.VMEM((SEQS, SLICE), bf16),
            pltpu.SMEM((BATCH,), jnp.int32),
            pltpu.VMEM((SEQS, SPAN, HEAD_SIZE), bf16),
            pltpu.VMEM((SEQS, SPAN, HEAD_SIZE), bf16),
            pltpu.VMEM((SEQS * HEADS, HEAD_SIZE), f32),
            pltpu.VMEM((SEQS, HEADS, SPAN), bf16),
            pltpu.VMEM((2 * SEQS * HEADS, HEAD_SIZE), f32),
            pltpu.VMEM((HEADS * 4, 8, 128), jnp.int32),
            pltpu.VMEM((CLANS, 8, 128), bf16),
            pltpu.VMEM((BATCH, 8, 128), bf16),
            pltpu.VMEM((GROUP, PIECE, SLICE), bf16),
            pltpu.VMEM((BATCH, SEQS, SLICE), bf16),
            pltpu.VMEM((BATCH, SEQS, SLICE), bf16),
            pltpu.VMEM((SEQS, 128), f32),
            pltpu.VMEM((TENSOR - 1, SEQS, 128), f32),
            pltpu.SemaphoreType.DMA((6,)),
            pltpu.SemaphoreType.DMA((SEQS,)),
            pltpu.SemaphoreType.DMA((SEQS,)),
        ]
        + [pltpu.SemaphoreType.DMA] * 3
        + [pltpu.SemaphoreType.DMA((BATCH // PART,))]
        + [pltpu.SemaphoreType.DMA] * 4,
        compiler_params=pltpu.CompilerParams(
            collective_id=0, has_side_effects=True, vmem_limit_bytes=56 * 1024 * 1024
        ),
    )(
        queries,
        fresh_key_heads,
        fresh_value_heads,
        cached_keys,
        value_cache_rows,
        lengths,
        residual,
        sectioned_rows,
        owners,
    )
    block = jax.ShapeDtypeStruct((SEQS, SLICE), bf16)
    out = pltpu.with_memory_space_constraint(out, pltpu.VMEM)
    return pl.pallas_call(finish, out_shape=(block, block))(out, norm_gain)


def solution(mesh):
    return jax.shard_map(
        local,
        mesh=mesh,
        in_specs=(
            P("batch", "tensor"),
            P("batch", "tensor"),
            P("batch", "tensor"),
            P("batch", "tensor", None, None),
            P("batch", "tensor", None, None),
            P("batch"),
            P("batch", "tensor"),
            P("batch", "tensor", None),
            P(),
            P("tensor"),
        ),
        out_specs=(P("batch", "tensor"), P("batch", "tensor")),
        check_vma=False,
    )
```

```python
import functools

import jax
import jax.numpy as jnp
from jax import lax
from jax.experimental import pallas as pl
from jax.experimental.pallas import tpu as pltpu
from jax.sharding import PartitionSpec as P

D = 5120
HEAD_SIZE = 128
HEADS = 8
SEQS = 4
SPAN = 4096
BATCH = 32
TENSOR = 8
GROUP = 8
CLANS = BATCH // GROUP
PART = BATCH // 4
PIECE = 32
SLICE = D // TENSOR
RECUT_ORDER = 0x1246357
MESH = pl.DeviceIdType.MESH


def place_of(batch):
    return ((batch >> 2 & 3) << 3) + ((batch >> 4) << 2) + (batch & 3)


def batch_of(place):
    return ((place >> 2 & 1) << 4) + ((place >> 3) << 2) + (place & 3)


def slice_of(member, tensor):
    step = 2 * (member & 1) + ((member >> 2) ^ (member >> 1 & 1))
    return ((tensor + 2 * step) & 7) ^ (member >> 1 & 1)


def batch_at(batch, step):
    ring, rest = step >> 2, 3 - (step & 3)
    away = 4 + ((ring + 1) >> 1) * (1 - 2 * (ring & 1))
    return ((batch & 16) ^ ((rest & 2) << 3)) + ((((batch & 15) + 2 * away) & 15) ^ (rest & 1))


def tensor_at(tensor, step):
    ring = step >> 1
    away = 2 + ((ring + 1) >> 1) * (1 - 2 * (ring & 1))
    return ((tensor + 2 * away) & 7) ^ (1 - (step & 1))


def slot_of(batch):
    return ((batch & 14) << 1) + ((batch >> 4) << 1) + (batch & 1)


def batch_of_slot(slot):
    return ((slot >> 1 & 1) << 4) + ((slot >> 2) << 1) + (slot & 1)


def kernel(
    q_hbm,
    fresh_k_hbm,
    fresh_v_hbm,
    keys_hbm,
    values_hbm,
    lengths_hbm,
    residual_hbm,
    rows_hbm,
    owners_hbm,
    gain_hbm,
    stream_ref,
    normed_ref,
    q_ref,
    fresh_k_ref,
    fresh_v_ref,
    lengths_ref,
    residual_ref,
    owners_ref,
    gain_ref,
    keys,
    values,
    q_by_head,
    weights,
    attended,
    goals,
    message,
    gathered,
    rows,
    partial,
    partials,
    square,
    squares,
    small_sem,
    key_sem,
    value_sem,
    rows_send,
    rows_recv,
    att_send,
    att_recv,
    part_send,
    part_recv,
    sq_send,
    sq_recv,
):
    batch, tensor = lax.axis_index("batch"), lax.axis_index("tensor")
    place = place_of(batch)
    clan, member = place >> 3, place & 7
    part = slice_of(member, tensor)
    mine = part == tensor
    late = (batch & 8) != 0

    small = [
        pltpu.make_async_copy(source, target, small_sem.at[i])
        for i, (source, target) in enumerate(
            (
                (q_hbm, q_ref),
                (fresh_k_hbm, fresh_k_ref),
                (fresh_v_hbm, fresh_v_ref),
                (lengths_hbm, lengths_ref),
                (owners_hbm, owners_ref),
                (residual_hbm, residual_ref),
                (gain_hbm, gain_ref),
            )
        )
    ]
    for copy in small:
        copy.start()
    for s in range(SEQS):
        pltpu.make_async_copy(keys_hbm.at[s, 0], keys.at[s], key_sem.at[s]).start()
    for s in range(SEQS):
        pltpu.make_async_copy(values_hbm.at[s, 0], values.at[s], value_sem.at[s]).start()


    barrier = pltpu.get_barrier_semaphore()

    def greet_batch(step, carry):
        pl.semaphore_signal(
            barrier, inc=1, device_id=(batch_at(batch, step), tensor), device_id_type=MESH
        )
        return carry

    def greet_tensor(step, carry):
        pl.semaphore_signal(
            barrier, inc=1, device_id=(batch, tensor_at(tensor, step)), device_id_type=MESH
        )
        return carry

    lax.fori_loop(0, 4, greet_batch, 0)
    lax.fori_loop(0, TENSOR - 1, greet_tensor, 0)
    lax.fori_loop(4, BATCH - 1, greet_batch, 0)

    def send_rows(step, carry):
        other = member ^ (RECUT_ORDER >> 4 * (step - 1) & 7)
        pltpu.make_async_remote_copy(
            src_ref=rows_hbm.at[0, :, pl.ds(pl.multiple_of(slice_of(other, tensor) * SLICE, 128), SLICE)],
            dst_ref=rows.at[member],
            send_sem=rows_send,
            recv_sem=rows_recv,
            device_id=(batch_of(clan * GROUP + other), tensor),
            device_id_type=MESH,
        ).start()
        return carry

    def open_up():
        pl.semaphore_wait(barrier, BATCH - 1 + TENSOR - 1)

    def recut():
        lax.fori_loop(1, GROUP, send_rows, 0)
        pltpu.make_async_copy(
            rows_hbm.at[0, :, pl.ds(pl.multiple_of(part * SLICE, 128), SLICE)],
            rows.at[member],
            rows_recv,
        ).start()


    for copy in small[:5]:
        copy.wait()

    row = lax.broadcasted_iota(jnp.int32, (8, 128), 0)
    lane = lax.broadcasted_iota(jnp.int32, (8, 128), 1)
    block = lane // PIECE
    code = (row // SEQS) * 4 + block
    for h in range(HEADS):
        targets = [place_of(owners_ref[4 * h + j]) for j in range(4)]
        for r in range(4):
            goal = jnp.full((8, 128), targets[(3 - r) % 4], jnp.int32)
            for j in range(3):
                goal = jnp.where(block == j, targets[(j - r) % 4], goal)
            goals[h * 4 + r] = goal - code

    q_all = q_ref[...].astype(jnp.float32)
    for h in range(HEADS):
        q_by_head[pl.ds(h, SEQS, stride=HEADS), :] = q_all[:, h * HEAD_SIZE : (h + 1) * HEAD_SIZE]
    fresh_k = fresh_k_ref[...].astype(jnp.float32)
    fresh_v = fresh_v_ref[...].astype(jnp.float32)
    scale = HEAD_SIZE ** (-0.5)
    position = lax.broadcasted_iota(jnp.int32, (HEADS, SPAN), 1)
    own_weights, totals = [], []
    for s in range(SEQS):
        if s == 2:
            @pl.when(late)
            def _():
                open_up()
                recut()

        if s % 2 == 0:
            for r in range(s, s + 2):
                pltpu.make_async_copy(keys_hbm.at[r, 0], keys.at[r], key_sem.at[r]).wait()
        q = q_by_head[s * HEADS : (s + 1) * HEADS, :]
        scores = (
            lax.dot_general(
                q.astype(jnp.bfloat16),
                keys[s],
                (((1,), (1,)), ((), ())),
                preferred_element_type=jnp.float32,
            )
            * scale
        )
        scores = jnp.where(position < lengths_ref[s], scores, -1e30)
        own = jnp.sum(q * fresh_k[s : s + 1, :], axis=1, keepdims=True) * scale
        top = jnp.maximum(jnp.max(scores, axis=1, keepdims=True), own)
        prob = jnp.exp(scores - top)
        own_prob = jnp.exp(own - top)
        totals.append(jnp.sum(prob, axis=1, keepdims=True) + own_prob)
        own_weights.append(own_prob.astype(jnp.bfloat16).astype(jnp.float32))
        weights[s] = prob.astype(jnp.bfloat16)

    for s in range(SEQS):
        pltpu.make_async_copy(values_hbm.at[s, 0], values.at[s], value_sem.at[s]).wait()
    for s in range(SEQS):
        mixed = lax.dot_general(
            weights[s], values[s], (((1,), (0,)), ((), ())), preferred_element_type=jnp.float32
        )
        mixed = (mixed + own_weights[s] * fresh_v[s : s + 1, :]) / totals[s]
        attended[s * HEADS : (s + 1) * HEADS, :] = mixed
        attended[(s + SEQS) * HEADS : (s + SEQS + 1) * HEADS, :] = mixed

    blocks = [jnp.zeros((8, 128), jnp.float32)] * CLANS
    for h in range(HEADS):
        head = attended[pl.ds(h, 8, stride=HEADS), :]
        for r in range(4):
            turned = pltpu.roll(head, r * PIECE, 1) if r else head
            goal = goals[h * 4 + r]
            blocks = [jnp.where(goal == c * GROUP, turned, blocks[c]) for c in range(CLANS)]
    for c in range(CLANS):
        message[c] = blocks[c].astype(jnp.bfloat16)

    slot = slot_of(batch)
    chunk = slot // PART

    def send_attended(step, carry):
        other = batch_at(batch, step)
        pltpu.make_async_remote_copy(
            src_ref=message.at[place_of(other) >> 3],
            dst_ref=gathered.at[slot],
            send_sem=att_send,
            recv_sem=att_recv.at[chunk],
            device_id=(other, tensor),
            device_id_type=MESH,
        ).start()
        return carry

    @pl.when(jnp.logical_not(late))
    def _():
        open_up()

    lax.fori_loop(0, BATCH - 1, send_attended, 0)
    pltpu.make_async_copy(message.at[clan], gathered.at[slot], att_recv.at[chunk]).start()

    @pl.when(jnp.logical_not(late))
    def _():
        recut()


    pltpu.make_async_copy(rows, rows, rows_recv).wait()


    def project(turn, carry):
        table = rows[...].reshape(GROUP * PIECE, SLICE)
        here = pl.ds(turn * PART, PART)
        pltpu.make_async_copy(gathered.at[here], gathered.at[here], att_recv.at[turn]).wait()
        first = gathered[here].astype(jnp.float32)
        swapped = pltpu.roll(first, SEQS, 1).reshape(PART * 8, 128).astype(jnp.bfloat16)
        first = first.reshape(PART * 8, 128).astype(jnp.bfloat16)
        product = jnp.dot(
            jnp.concatenate([first, swapped], axis=1), table, preferred_element_type=jnp.float32
        )
        partial[here] = product.reshape(PART, 8, SLICE)[:, :SEQS].astype(jnp.bfloat16)

        def send_partial(step, carry):
            other = turn * PART + step
            local = mine & (other == slot)

            @pl.when(jnp.logical_not(local))
            def _():
                pltpu.make_async_remote_copy(
                    src_ref=partial.at[other],
                    dst_ref=partials.at[tensor * CLANS + clan],
                    send_sem=part_send,
                    recv_sem=part_recv,
                    device_id=(batch_of_slot(other), part),
                    device_id_type=MESH,
                ).start()

            @pl.when(local)
            def _():
                pltpu.make_async_copy(
                    partial.at[other], partials.at[tensor * CLANS + clan], part_recv
                ).start()

            return carry

        lax.fori_loop(0, PART, send_partial, 0)
        return carry

    lax.fori_loop(0, BATCH // PART, project, 0)
    for copy in small[5:]:
        copy.wait()
    pltpu.make_async_copy(partials, partials, part_recv).wait()
    total = jnp.sum(partials[...].astype(jnp.float32), axis=0)
    stream = residual_ref[...].astype(jnp.float32) + total

    squared = jnp.sum(stream * stream, axis=1, keepdims=True)
    square[...] = jnp.broadcast_to(squared, (SEQS, 128))

    def send_square(step, carry):
        pltpu.make_async_remote_copy(
            src_ref=square,
            dst_ref=squares.at[step],
            send_sem=sq_send,
            recv_sem=sq_recv,
            device_id=(batch, tensor_at(tensor, step)),
            device_id_type=MESH,
        ).start()
        return carry

    lax.fori_loop(0, TENSOR - 1, send_square, 0)

    stream_ref[...] = stream.astype(jnp.bfloat16)
    scaled = stream * gain_ref[...].astype(jnp.float32).reshape(1, SLICE)
    pltpu.make_async_copy(squares, squares, sq_recv).wait()
    mean = (squared + jnp.sum(squares[...], axis=0)[:, :1]) / D
    inverse = lax.rsqrt(mean + 1e-6)
    normed_ref[...] = (scaled * inverse).astype(jnp.bfloat16)

    pltpu.make_async_copy(squares, squares, sq_send).wait()
    pltpu.make_async_copy(rows.at[: GROUP - 1], rows.at[: GROUP - 1], rows_send).wait()
    pltpu.make_async_copy(gathered.at[: BATCH - 1], gathered.at[: BATCH - 1], att_send).wait()
    pltpu.make_async_copy(partial.at[: BATCH - 1], partial.at[: BATCH - 1], part_send).wait()

    @pl.when(jnp.logical_not(mine))
    def _():
        pltpu.make_async_copy(partial.at[0], partial.at[0], part_send).wait()


def finish(stream_ref, normed_ref, stream_hbm, normed_hbm, sem):
    copies = [
        pltpu.make_async_copy(stream_ref, stream_hbm, sem.at[0]),
        pltpu.make_async_copy(normed_ref, normed_hbm, sem.at[1]),
    ]
    for copy in copies:
        copy.start()
    for copy in copies:
        copy.wait()


def local(
    queries,
    fresh_key_heads,
    fresh_value_heads,
    cached_keys,
    value_cache_rows,
    lengths,
    residual,
    sectioned_rows,
    owners,
    norm_gain,
):
    anywhere = pl.BlockSpec(memory_space=pl.ANY)
    bf16, f32 = jnp.bfloat16, jnp.float32
    outs = pl.pallas_call(
        kernel,
        out_shape=(pltpu.VMEM((SEQS, SLICE), bf16),) * 2,
        in_specs=[anywhere] * 10,
        out_specs=(pl.BlockSpec(memory_space=pltpu.VMEM),) * 2,
        scratch_shapes=[
            pltpu.VMEM((SEQS, HEADS * HEAD_SIZE), bf16),
            pltpu.VMEM((SEQS, HEAD_SIZE), bf16),
            pltpu.VMEM((SEQS, HEAD_SIZE), bf16),
            pltpu.SMEM((SEQS,), jnp.int32),
            pltpu.VMEM((SEQS, SLICE), bf16),
            pltpu.SMEM((BATCH,), jnp.int32),
            pltpu.VMEM((SLICE,), bf16),
            pltpu.VMEM((SEQS, SPAN, HEAD_SIZE), bf16),
            pltpu.VMEM((SEQS, SPAN, HEAD_SIZE), bf16),
            pltpu.VMEM((SEQS * HEADS, HEAD_SIZE), f32),
            pltpu.VMEM((SEQS, HEADS, SPAN), bf16),
            pltpu.VMEM((2 * SEQS * HEADS, HEAD_SIZE), f32),
            pltpu.VMEM((HEADS * 4, 8, 128), jnp.int32),
            pltpu.VMEM((CLANS, 8, 128), bf16),
            pltpu.VMEM((BATCH, 8, 128), bf16),
            pltpu.VMEM((GROUP, PIECE, SLICE), bf16),
            pltpu.VMEM((BATCH, SEQS, SLICE), bf16),
            pltpu.VMEM((BATCH, SEQS, SLICE), bf16),
            pltpu.VMEM((SEQS, 128), f32),
            pltpu.VMEM((TENSOR - 1, SEQS, 128), f32),
            pltpu.SemaphoreType.DMA((7,)),
            pltpu.SemaphoreType.DMA((SEQS,)),
            pltpu.SemaphoreType.DMA((SEQS,)),
        ]
        + [pltpu.SemaphoreType.DMA] * 3
        + [pltpu.SemaphoreType.DMA((BATCH // PART,))]
        + [pltpu.SemaphoreType.DMA] * 4,
        compiler_params=pltpu.CompilerParams(
            collective_id=0, has_side_effects=True, vmem_limit_bytes=56 * 1024 * 1024
        ),
    )(
        queries,
        fresh_key_heads,
        fresh_value_heads,
        cached_keys,
        value_cache_rows,
        lengths,
        residual,
        sectioned_rows,
        owners,
        norm_gain,
    )
    block = jax.ShapeDtypeStruct((SEQS, SLICE), bf16)
    return pl.pallas_call(
        finish,
        out_shape=(block, block),
        in_specs=[pl.BlockSpec(memory_space=pltpu.VMEM)] * 2,
        out_specs=(anywhere, anywhere),
        scratch_shapes=[pltpu.SemaphoreType.DMA((2,))],
    )(*[pltpu.with_memory_space_constraint(x, pltpu.VMEM) for x in outs])
    block = jax.ShapeDtypeStruct((SEQS, SLICE), bf16)


def solution(mesh):
    return jax.shard_map(
        local,
        mesh=mesh,
        in_specs=(
            P("batch", "tensor"),
            P("batch", "tensor"),
            P("batch", "tensor"),
            P("batch", "tensor", None, None),
            P("batch", "tensor", None, None),
            P("batch"),
            P("batch", "tensor"),
            P("batch", "tensor", None),
            P(),
            P("tensor"),
        ),
        out_specs=(P("batch", "tensor"), P("batch", "tensor")),
        check_vma=False,
    )
```

```python
import functools

import jax
import jax.numpy as jnp
from jax import lax
from jax.experimental import pallas as pl
from jax.experimental.pallas import tpu as pltpu
from jax.sharding import PartitionSpec as P

D = 5120
HEAD_SIZE = 128
HEADS = 8
SEQS = 4
SPAN = 4096
BATCH = 32
TENSOR = 8
GROUP = 8
CLANS = BATCH // GROUP
PART = BATCH // 4
PIECE = 32
SLICE = D // TENSOR
RECUT_ORDER = 0x2461357
MESH = pl.DeviceIdType.MESH


def place_of(batch):
    return ((batch >> 2 & 3) << 3) + ((batch >> 4) << 2) + (batch & 3)


def batch_of(place):
    return ((place >> 2 & 1) << 4) + ((place >> 3) << 2) + (place & 3)


def slice_of(member, tensor):
    step = 2 * (member & 1) + (member >> 1 & 1)
    return ((tensor + 2 * step) & 7) ^ (member >> 2)


def batch_at(batch, step):
    ring, rest = step >> 2, 3 - (step & 3)
    away = 4 + ((ring + 1) >> 1) * (1 - 2 * (ring & 1))
    return ((batch & 16) ^ ((rest & 2) << 3)) + ((((batch & 15) + 2 * away) & 15) ^ (rest & 1))


def tensor_at(tensor, step):
    ring = step >> 1
    away = 2 + ((ring + 1) >> 1) * (1 - 2 * (ring & 1))
    return ((tensor + 2 * away) & 7) ^ (1 - (step & 1))


def slot_of(batch):
    return ((batch & 14) << 1) + ((batch >> 4) << 1) + (batch & 1)


def batch_of_slot(slot):
    return ((slot >> 1 & 1) << 4) + ((slot >> 2) << 1) + (slot & 1)


def kernel(
    q_hbm,
    fresh_k_hbm,
    fresh_v_hbm,
    keys_hbm,
    values_hbm,
    lengths_hbm,
    residual_hbm,
    rows_hbm,
    owners_hbm,
    gain_hbm,
    stream_ref,
    normed_ref,
    q_ref,
    fresh_k_ref,
    fresh_v_ref,
    lengths_ref,
    residual_ref,
    owners_ref,
    gain_ref,
    keys,
    values,
    q_by_head,
    weights,
    attended,
    goals,
    message,
    gathered,
    staged,
    rows,
    partial,
    partials,
    square,
    squares,
    small_sem,
    staged_sem,
    key_sem,
    value_sem,
    rows_send,
    rows_recv,
    att_send,
    att_recv,
    part_send,
    part_recv,
    sq_send,
    sq_recv,
):
    batch, tensor = lax.axis_index("batch"), lax.axis_index("tensor")
    place = place_of(batch)
    clan, member = place >> 3, place & 7
    part = slice_of(member, tensor)
    mine = part == tensor
    late = (batch & 8) != 0

    small = [
        pltpu.make_async_copy(source, target, small_sem.at[i])
        for i, (source, target) in enumerate(
            (
                (q_hbm, q_ref),
                (fresh_k_hbm, fresh_k_ref),
                (fresh_v_hbm, fresh_v_ref),
                (lengths_hbm, lengths_ref),
                (owners_hbm, owners_ref),
                (residual_hbm, residual_ref),
                (gain_hbm, gain_ref),
            )
        )
    ]
    for copy in small:
        copy.start()
    for s in range(SEQS):
        pltpu.make_async_copy(keys_hbm.at[s, 0], keys.at[s], key_sem.at[s]).start()
    pltpu.make_async_copy(rows_hbm.at[0], staged, staged_sem).start()
    for s in range(SEQS):
        pltpu.make_async_copy(values_hbm.at[s, 0], values.at[s], value_sem.at[s]).start()


    barrier = pltpu.get_barrier_semaphore()

    def greet_batch(step, carry):
        pl.semaphore_signal(
            barrier, inc=1, device_id=(batch_at(batch, step), tensor), device_id_type=MESH
        )
        return carry

    def greet_tensor(step, carry):
        pl.semaphore_signal(
            barrier, inc=1, device_id=(batch, tensor_at(tensor, step)), device_id_type=MESH
        )
        return carry

    lax.fori_loop(0, 4, greet_batch, 0)
    lax.fori_loop(0, TENSOR - 1, greet_tensor, 0)
    lax.fori_loop(4, BATCH - 1, greet_batch, 0)

    def send_rows(step, carry):
        other = member ^ (RECUT_ORDER >> 4 * (step - 1) & 7)
        pltpu.make_async_remote_copy(
            src_ref=staged.at[:, pl.ds(pl.multiple_of(slice_of(other, tensor) * SLICE, 128), SLICE)],
            dst_ref=rows.at[member],
            send_sem=rows_send,
            recv_sem=rows_recv,
            device_id=(batch_of(clan * GROUP + other), tensor),
            device_id_type=MESH,
        ).start()
        return carry

    def open_up():
        pl.semaphore_wait(barrier, BATCH - 1 + TENSOR - 1)

    def recut():
        pltpu.make_async_copy(rows_hbm.at[0], staged, staged_sem).wait()
        lax.fori_loop(1, GROUP, send_rows, 0)
        pltpu.make_async_copy(
            staged.at[:, pl.ds(pl.multiple_of(part * SLICE, 128), SLICE)],
            rows.at[member],
            rows_recv,
        ).start()


    for copy in small[:5]:
        copy.wait()

    row = lax.broadcasted_iota(jnp.int32, (8, 128), 0)
    lane = lax.broadcasted_iota(jnp.int32, (8, 128), 1)
    block = lane // PIECE
    code = (row // SEQS) * 4 + block
    for h in range(HEADS):
        targets = [place_of(owners_ref[4 * h + j]) for j in range(4)]
        for r in range(4):
            goal = jnp.full((8, 128), targets[(3 - r) % 4], jnp.int32)
            for j in range(3):
                goal = jnp.where(block == j, targets[(j - r) % 4], goal)
            goals[h * 4 + r] = goal - code

    q_all = q_ref[...].astype(jnp.float32)
    for h in range(HEADS):
        q_by_head[pl.ds(h, SEQS, stride=HEADS), :] = q_all[:, h * HEAD_SIZE : (h + 1) * HEAD_SIZE]
    fresh_k = fresh_k_ref[...].astype(jnp.float32)
    fresh_v = fresh_v_ref[...].astype(jnp.float32)
    scale = HEAD_SIZE ** (-0.5)
    position = lax.broadcasted_iota(jnp.int32, (HEADS, SPAN), 1)
    own_weights, totals = [], []
    for s in range(SEQS):
        if s == 2:
            @pl.when(late)
            def _():
                open_up()
                recut()

        if s % 2 == 0:
            for r in range(s, s + 2):
                pltpu.make_async_copy(keys_hbm.at[r, 0], keys.at[r], key_sem.at[r]).wait()
        q = q_by_head[s * HEADS : (s + 1) * HEADS, :]
        scores = (
            lax.dot_general(
                q.astype(jnp.bfloat16),
                keys[s],
                (((1,), (1,)), ((), ())),
                preferred_element_type=jnp.float32,
            )
            * scale
        )
        scores = jnp.where(position < lengths_ref[s], scores, -1e30)
        own = jnp.sum(q * fresh_k[s : s + 1, :], axis=1, keepdims=True) * scale
        top = jnp.maximum(jnp.max(scores, axis=1, keepdims=True), own)
        prob = jnp.exp(scores - top)
        own_prob = jnp.exp(own - top)
        totals.append(jnp.sum(prob, axis=1, keepdims=True) + own_prob)
        own_weights.append(own_prob.astype(jnp.bfloat16).astype(jnp.float32))
        weights[s] = prob.astype(jnp.bfloat16)

    for s in range(SEQS):
        pltpu.make_async_copy(values_hbm.at[s, 0], values.at[s], value_sem.at[s]).wait()
    for s in range(SEQS):
        mixed = lax.dot_general(
            weights[s], values[s], (((1,), (0,)), ((), ())), preferred_element_type=jnp.float32
        )
        mixed = (mixed + own_weights[s] * fresh_v[s : s + 1, :]) / totals[s]
        attended[s * HEADS : (s + 1) * HEADS, :] = mixed
        attended[(s + SEQS) * HEADS : (s + SEQS + 1) * HEADS, :] = mixed

    blocks = [jnp.zeros((8, 128), jnp.float32)] * CLANS
    for h in range(HEADS):
        head = attended[pl.ds(h, 8, stride=HEADS), :]
        for r in range(4):
            turned = pltpu.roll(head, r * PIECE, 1) if r else head
            goal = goals[h * 4 + r]
            blocks = [jnp.where(goal == c * GROUP, turned, blocks[c]) for c in range(CLANS)]
    for c in range(CLANS):
        message[c] = blocks[c].astype(jnp.bfloat16)

    slot = slot_of(batch)
    chunk = slot // PART

    def send_attended(step, carry):
        other = batch_at(batch, step)
        pltpu.make_async_remote_copy(
            src_ref=message.at[place_of(other) >> 3],
            dst_ref=gathered.at[slot],
            send_sem=att_send,
            recv_sem=att_recv.at[chunk],
            device_id=(other, tensor),
            device_id_type=MESH,
        ).start()
        return carry

    @pl.when(jnp.logical_not(late))
    def _():
        open_up()

    lax.fori_loop(0, BATCH - 1, send_attended, 0)
    pltpu.make_async_copy(message.at[clan], gathered.at[slot], att_recv.at[chunk]).start()

    @pl.when(jnp.logical_not(late))
    def _():
        recut()


    pltpu.make_async_copy(rows, rows, rows_recv).wait()


    def project(turn, carry):
        table = rows[...].reshape(GROUP * PIECE, SLICE)
        here = pl.ds(turn * PART, PART)
        pltpu.make_async_copy(gathered.at[here], gathered.at[here], att_recv.at[turn]).wait()
        first = gathered[here].astype(jnp.float32)
        swapped = pltpu.roll(first, SEQS, 1).reshape(PART * 8, 128).astype(jnp.bfloat16)
        first = first.reshape(PART * 8, 128).astype(jnp.bfloat16)
        product = jnp.dot(
            jnp.concatenate([first, swapped], axis=1), table, preferred_element_type=jnp.float32
        )
        partial[here] = product.reshape(PART, 8, SLICE)[:, :SEQS].astype(jnp.bfloat16)

        def send_partial(step, carry):
            other = turn * PART + step
            local = mine & (other == slot)

            @pl.when(jnp.logical_not(local))
            def _():
                pltpu.make_async_remote_copy(
                    src_ref=partial.at[other],
                    dst_ref=partials.at[tensor * CLANS + clan],
                    send_sem=part_send,
                    recv_sem=part_recv,
                    device_id=(batch_of_slot(other), part),
                    device_id_type=MESH,
                ).start()

            @pl.when(local)
            def _():
                pltpu.make_async_copy(
                    partial.at[other], partials.at[tensor * CLANS + clan], part_recv
                ).start()

            return carry

        lax.fori_loop(0, PART, send_partial, 0)
        return carry

    lax.fori_loop(0, BATCH // PART, project, 0)
    for copy in small[5:]:
        copy.wait()
    pltpu.make_async_copy(partials, partials, part_recv).wait()
    total = jnp.sum(partials[...].astype(jnp.float32), axis=0)
    stream = residual_ref[...].astype(jnp.float32) + total

    squared = jnp.sum(stream * stream, axis=1, keepdims=True)
    square[...] = jnp.broadcast_to(squared, (SEQS, 128))

    def send_square(step, carry):
        pltpu.make_async_remote_copy(
            src_ref=square,
            dst_ref=squares.at[step],
            send_sem=sq_send,
            recv_sem=sq_recv,
            device_id=(batch, tensor_at(tensor, step)),
            device_id_type=MESH,
        ).start()
        return carry

    lax.fori_loop(0, TENSOR - 1, send_square, 0)

    stream_ref[...] = stream.astype(jnp.bfloat16)
    scaled = stream * gain_ref[...].astype(jnp.float32).reshape(1, SLICE)
    pltpu.make_async_copy(squares, squares, sq_recv).wait()
    mean = (squared + jnp.sum(squares[...], axis=0)[:, :1]) / D
    inverse = lax.rsqrt(mean + 1e-6)
    normed_ref[...] = (scaled * inverse).astype(jnp.bfloat16)

    pltpu.make_async_copy(squares, squares, sq_send).wait()
    pltpu.make_async_copy(rows.at[: GROUP - 1], rows.at[: GROUP - 1], rows_send).wait()
    pltpu.make_async_copy(gathered.at[: BATCH - 1], gathered.at[: BATCH - 1], att_send).wait()
    pltpu.make_async_copy(partial.at[: BATCH - 1], partial.at[: BATCH - 1], part_send).wait()

    @pl.when(jnp.logical_not(mine))
    def _():
        pltpu.make_async_copy(partial.at[0], partial.at[0], part_send).wait()


def finish(stream_ref, normed_ref, stream_hbm, normed_hbm, sem):
    copies = [
        pltpu.make_async_copy(stream_ref, stream_hbm, sem.at[0]),
        pltpu.make_async_copy(normed_ref, normed_hbm, sem.at[1]),
    ]
    for copy in copies:
        copy.start()
    for copy in copies:
        copy.wait()


def local(
    queries,
    fresh_key_heads,
    fresh_value_heads,
    cached_keys,
    value_cache_rows,
    lengths,
    residual,
    sectioned_rows,
    owners,
    norm_gain,
):
    anywhere = pl.BlockSpec(memory_space=pl.ANY)
    bf16, f32 = jnp.bfloat16, jnp.float32
    outs = pl.pallas_call(
        kernel,
        out_shape=(pltpu.VMEM((SEQS, SLICE), bf16),) * 2,
        in_specs=[anywhere] * 10,
        out_specs=(pl.BlockSpec(memory_space=pltpu.VMEM),) * 2,
        scratch_shapes=[
            pltpu.VMEM((SEQS, HEADS * HEAD_SIZE), bf16),
            pltpu.VMEM((SEQS, HEAD_SIZE), bf16),
            pltpu.VMEM((SEQS, HEAD_SIZE), bf16),
            pltpu.SMEM((SEQS,), jnp.int32),
            pltpu.VMEM((SEQS, SLICE), bf16),
            pltpu.SMEM((BATCH,), jnp.int32),
            pltpu.VMEM((SLICE,), bf16),
            pltpu.VMEM((SEQS, SPAN, HEAD_SIZE), bf16),
            pltpu.VMEM((SEQS, SPAN, HEAD_SIZE), bf16),
            pltpu.VMEM((SEQS * HEADS, HEAD_SIZE), f32),
            pltpu.VMEM((SEQS, HEADS, SPAN), bf16),
            pltpu.VMEM((2 * SEQS * HEADS, HEAD_SIZE), f32),
            pltpu.VMEM((HEADS * 4, 8, 128), jnp.int32),
            pltpu.VMEM((CLANS, 8, 128), bf16),
            pltpu.VMEM((BATCH, 8, 128), bf16),
            pltpu.VMEM((PIECE, D), bf16),
            pltpu.VMEM((GROUP, PIECE, SLICE), bf16),
            pltpu.VMEM((BATCH, SEQS, SLICE), bf16),
            pltpu.VMEM((BATCH, SEQS, SLICE), bf16),
            pltpu.VMEM((SEQS, 128), f32),
            pltpu.VMEM((TENSOR - 1, SEQS, 128), f32),
            pltpu.SemaphoreType.DMA((7,)),
            pltpu.SemaphoreType.DMA,
            pltpu.SemaphoreType.DMA((SEQS,)),
            pltpu.SemaphoreType.DMA((SEQS,)),
        ]
        + [pltpu.SemaphoreType.DMA] * 3
        + [pltpu.SemaphoreType.DMA((BATCH // PART,))]
        + [pltpu.SemaphoreType.DMA] * 4,
        compiler_params=pltpu.CompilerParams(
            collective_id=0, has_side_effects=True, vmem_limit_bytes=56 * 1024 * 1024
        ),
    )(
        queries,
        fresh_key_heads,
        fresh_value_heads,
        cached_keys,
        value_cache_rows,
        lengths,
        residual,
        sectioned_rows,
        owners,
        norm_gain,
    )
    block = jax.ShapeDtypeStruct((SEQS, SLICE), bf16)
    return pl.pallas_call(
        finish,
        out_shape=(block, block),
        in_specs=[pl.BlockSpec(memory_space=pltpu.VMEM)] * 2,
        out_specs=(anywhere, anywhere),
        scratch_shapes=[pltpu.SemaphoreType.DMA((2,))],
    )(*[pltpu.with_memory_space_constraint(x, pltpu.VMEM) for x in outs])
    block = jax.ShapeDtypeStruct((SEQS, SLICE), bf16)


def solution(mesh):
    return jax.shard_map(
        local,
        mesh=mesh,
        in_specs=(
            P("batch", "tensor"),
            P("batch", "tensor"),
            P("batch", "tensor"),
            P("batch", "tensor", None, None),
            P("batch", "tensor", None, None),
            P("batch"),
            P("batch", "tensor"),
            P("batch", "tensor", None),
            P(),
            P("tensor"),
        ),
        out_specs=(P("batch", "tensor"), P("batch", "tensor")),
        check_vma=False,
    )
```

```python
import functools

import jax
import jax.numpy as jnp
from jax import lax
from jax.experimental import pallas as pl
from jax.experimental.pallas import tpu as pltpu
from jax.sharding import PartitionSpec as P

D = 5120
HEAD_SIZE = 128
HEADS = 8
SEQS = 4
SPAN = 4096
BATCH = 32
TENSOR = 8
GROUP = 8
CLANS = BATCH // GROUP
PART = BATCH // 4
PIECE = 32
SLICE = D // TENSOR
RECUT_ORDER = 0x4261537
MESH = pl.DeviceIdType.MESH


def place_of(batch):
    return ((batch >> 2 & 3) << 3) + ((batch >> 4) << 2) + (batch & 3)


def batch_of(place):
    return ((place >> 2 & 1) << 4) + ((place >> 3) << 2) + (place & 3)


def slice_of(member, tensor):
    step = 2 * (member & 1) + (member >> 1 & 1)
    return ((tensor + 2 * step) & 7) ^ (member >> 2)


def batch_at(batch, step):
    ring, rest = step >> 2, 3 - (step & 3)
    side = 1 - 2 * (batch & 1)
    away = 4 + side * ((ring + 1) >> 1) * (1 - 2 * (ring & 1))
    return ((batch & 16) ^ ((rest & 2) << 3)) + ((((batch & 15) + 2 * away) & 15) ^ (rest & 1))


def tensor_at(tensor, step):
    ring = step >> 1
    away = 2 + ((ring + 1) >> 1) * (1 - 2 * (ring & 1))
    return ((tensor + 2 * away) & 7) ^ (1 - (step & 1))


def slot_of(batch):
    return ((batch & 14) << 1) + ((batch >> 4) << 1) + (batch & 1)


def batch_of_slot(slot):
    return ((slot >> 1 & 1) << 4) + ((slot >> 2) << 1) + (slot & 1)


def kernel(
    q_hbm,
    fresh_k_hbm,
    fresh_v_hbm,
    keys_hbm,
    values_hbm,
    lengths_hbm,
    residual_hbm,
    rows_hbm,
    owners_hbm,
    gain_hbm,
    stream_ref,
    normed_ref,
    q_ref,
    fresh_k_ref,
    fresh_v_ref,
    lengths_ref,
    residual_ref,
    owners_ref,
    gain_ref,
    keys,
    values,
    q_by_head,
    weights,
    attended,
    goals,
    message,
    gathered,
    staged,
    rows,
    partial,
    partials,
    square,
    squares,
    small_sem,
    staged_sem,
    key_sem,
    value_sem,
    rows_send,
    rows_recv,
    att_send,
    att_recv,
    part_send,
    part_recv,
    sq_send,
    sq_recv,
):
    batch, tensor = lax.axis_index("batch"), lax.axis_index("tensor")
    place = place_of(batch)
    clan, member = place >> 3, place & 7
    part = slice_of(member, tensor)
    mine = part == tensor
    late = (batch & 8) != 0

    small = [
        pltpu.make_async_copy(source, target, small_sem.at[i])
        for i, (source, target) in enumerate(
            (
                (q_hbm, q_ref),
                (fresh_k_hbm, fresh_k_ref),
                (fresh_v_hbm, fresh_v_ref),
                (lengths_hbm, lengths_ref),
                (owners_hbm, owners_ref),
                (residual_hbm, residual_ref),
                (gain_hbm, gain_ref),
            )
        )
    ]
    for copy in small:
        copy.start()
    for s in range(SEQS):
        pltpu.make_async_copy(keys_hbm.at[s, 0], keys.at[s], key_sem.at[s]).start()
    pltpu.make_async_copy(rows_hbm.at[0], staged, staged_sem).start()
    for s in range(SEQS):
        pltpu.make_async_copy(values_hbm.at[s, 0], values.at[s], value_sem.at[s]).start()


    barrier = pltpu.get_barrier_semaphore()

    def greet_batch(step, carry):
        pl.semaphore_signal(
            barrier, inc=1, device_id=(batch_at(batch, step), tensor), device_id_type=MESH
        )
        return carry

    def greet_tensor(step, carry):
        pl.semaphore_signal(
            barrier, inc=1, device_id=(batch, tensor_at(tensor, step)), device_id_type=MESH
        )
        return carry

    lax.fori_loop(0, 4, greet_batch, 0)
    lax.fori_loop(0, TENSOR - 1, greet_tensor, 0)
    lax.fori_loop(4, BATCH - 1, greet_batch, 0)

    def send_rows(step, carry):
        other = member ^ (RECUT_ORDER >> 4 * (step - 1) & 7)
        pltpu.make_async_remote_copy(
            src_ref=staged.at[:, pl.ds(pl.multiple_of(slice_of(other, tensor) * SLICE, 128), SLICE)],
            dst_ref=rows.at[member],
            send_sem=rows_send,
            recv_sem=rows_recv,
            device_id=(batch_of(clan * GROUP + other), tensor),
            device_id_type=MESH,
        ).start()
        return carry

    def open_up():
        pl.semaphore_wait(barrier, BATCH - 1 + TENSOR - 1)

    def recut():
        pltpu.make_async_copy(rows_hbm.at[0], staged, staged_sem).wait()
        lax.fori_loop(1, GROUP, send_rows, 0)
        pltpu.make_async_copy(
            staged.at[:, pl.ds(pl.multiple_of(part * SLICE, 128), SLICE)],
            rows.at[member],
            rows_recv,
        ).start()


    for copy in small[:5]:
        copy.wait()

    row = lax.broadcasted_iota(jnp.int32, (8, 128), 0)
    lane = lax.broadcasted_iota(jnp.int32, (8, 128), 1)
    block = lane // PIECE
    code = (row // SEQS) * 4 + block
    for h in range(HEADS):
        targets = [place_of(owners_ref[4 * h + j]) for j in range(4)]
        for r in range(4):
            goal = jnp.full((8, 128), targets[(3 - r) % 4], jnp.int32)
            for j in range(3):
                goal = jnp.where(block == j, targets[(j - r) % 4], goal)
            goals[h * 4 + r] = goal - code

    q_all = q_ref[...].astype(jnp.float32)
    for h in range(HEADS):
        q_by_head[pl.ds(h, SEQS, stride=HEADS), :] = q_all[:, h * HEAD_SIZE : (h + 1) * HEAD_SIZE]
    fresh_k = fresh_k_ref[...].astype(jnp.float32)
    fresh_v = fresh_v_ref[...].astype(jnp.float32)
    scale = HEAD_SIZE ** (-0.5)
    position = lax.broadcasted_iota(jnp.int32, (HEADS, SPAN), 1)
    own_weights, totals = [], []
    for s in range(SEQS):
        if s == 2:
            @pl.when(late)
            def _():
                open_up()
                recut()

        if s % 2 == 0:
            for r in range(s, s + 2):
                pltpu.make_async_copy(keys_hbm.at[r, 0], keys.at[r], key_sem.at[r]).wait()
        q = q_by_head[s * HEADS : (s + 1) * HEADS, :]
        scores = (
            lax.dot_general(
                q.astype(jnp.bfloat16),
                keys[s],
                (((1,), (1,)), ((), ())),
                preferred_element_type=jnp.float32,
            )
            * scale
        )
        scores = jnp.where(position < lengths_ref[s], scores, -1e30)
        own = jnp.sum(q * fresh_k[s : s + 1, :], axis=1, keepdims=True) * scale
        top = jnp.maximum(jnp.max(scores, axis=1, keepdims=True), own)
        prob = jnp.exp(scores - top)
        own_prob = jnp.exp(own - top)
        totals.append(jnp.sum(prob, axis=1, keepdims=True) + own_prob)
        own_weights.append(own_prob.astype(jnp.bfloat16).astype(jnp.float32))
        weights[s] = prob.astype(jnp.bfloat16)

    for s in range(SEQS):
        pltpu.make_async_copy(values_hbm.at[s, 0], values.at[s], value_sem.at[s]).wait()
    for s in range(SEQS):
        mixed = lax.dot_general(
            weights[s], values[s], (((1,), (0,)), ((), ())), preferred_element_type=jnp.float32
        )
        mixed = (mixed + own_weights[s] * fresh_v[s : s + 1, :]) / totals[s]
        attended[s * HEADS : (s + 1) * HEADS, :] = mixed
        attended[(s + SEQS) * HEADS : (s + SEQS + 1) * HEADS, :] = mixed

    blocks = [jnp.zeros((8, 128), jnp.float32)] * CLANS
    for h in range(HEADS):
        head = attended[pl.ds(h, 8, stride=HEADS), :]
        for r in range(4):
            turned = pltpu.roll(head, r * PIECE, 1) if r else head
            goal = goals[h * 4 + r]
            blocks = [jnp.where(goal == c * GROUP, turned, blocks[c]) for c in range(CLANS)]
    for c in range(CLANS):
        message[c] = blocks[c].astype(jnp.bfloat16)

    slot = slot_of(batch)
    chunk = slot // PART

    def send_attended(step, carry):
        other = batch_at(batch, step)
        pltpu.make_async_remote_copy(
            src_ref=message.at[place_of(other) >> 3],
            dst_ref=gathered.at[slot],
            send_sem=att_send,
            recv_sem=att_recv.at[chunk],
            device_id=(other, tensor),
            device_id_type=MESH,
        ).start()
        return carry

    @pl.when(jnp.logical_not(late))
    def _():
        open_up()

    lax.fori_loop(0, BATCH - 1, send_attended, 0)
    pltpu.make_async_copy(message.at[clan], gathered.at[slot], att_recv.at[chunk]).start()

    @pl.when(jnp.logical_not(late))
    def _():
        recut()


    pltpu.make_async_copy(rows, rows, rows_recv).wait()


    def project(turn, carry):
        table = rows[...].reshape(GROUP * PIECE, SLICE)
        here = pl.ds(turn * PART, PART)
        pltpu.make_async_copy(gathered.at[here], gathered.at[here], att_recv.at[turn]).wait()
        first = gathered[here].astype(jnp.float32)
        swapped = pltpu.roll(first, SEQS, 1).reshape(PART * 8, 128).astype(jnp.bfloat16)
        first = first.reshape(PART * 8, 128).astype(jnp.bfloat16)
        product = jnp.dot(
            jnp.concatenate([first, swapped], axis=1), table, preferred_element_type=jnp.float32
        )
        partial[here] = product.reshape(PART, 8, SLICE)[:, :SEQS].astype(jnp.bfloat16)

        def send_partial(step, carry):
            other = turn * PART + step
            local = mine & (other == slot)

            @pl.when(jnp.logical_not(local))
            def _():
                pltpu.make_async_remote_copy(
                    src_ref=partial.at[other],
                    dst_ref=partials.at[tensor * CLANS + clan],
                    send_sem=part_send,
                    recv_sem=part_recv,
                    device_id=(batch_of_slot(other), part),
                    device_id_type=MESH,
                ).start()

            @pl.when(local)
            def _():
                pltpu.make_async_copy(
                    partial.at[other], partials.at[tensor * CLANS + clan], part_recv
                ).start()

            return carry

        lax.fori_loop(0, PART, send_partial, 0)
        return carry

    lax.fori_loop(0, BATCH // PART, project, 0)
    for copy in small[5:]:
        copy.wait()
    pltpu.make_async_copy(partials, partials, part_recv).wait()
    total = jnp.sum(partials[...].astype(jnp.float32), axis=0)
    stream = residual_ref[...].astype(jnp.float32) + total

    squared = jnp.sum(stream * stream, axis=1, keepdims=True)
    square[...] = jnp.broadcast_to(squared, (SEQS, 128))

    def send_square(step, carry):
        pltpu.make_async_remote_copy(
            src_ref=square,
            dst_ref=squares.at[step],
            send_sem=sq_send,
            recv_sem=sq_recv,
            device_id=(batch, tensor_at(tensor, step)),
            device_id_type=MESH,
        ).start()
        return carry

    lax.fori_loop(0, TENSOR - 1, send_square, 0)

    stream_ref[...] = stream.astype(jnp.bfloat16)
    scaled = stream * gain_ref[...].astype(jnp.float32).reshape(1, SLICE)
    pltpu.make_async_copy(rows.at[: GROUP - 1], rows.at[: GROUP - 1], rows_send).wait()
    pltpu.make_async_copy(gathered.at[: BATCH - 1], gathered.at[: BATCH - 1], att_send).wait()
    pltpu.make_async_copy(partial.at[: BATCH - 1], partial.at[: BATCH - 1], part_send).wait()

    @pl.when(jnp.logical_not(mine))
    def _():
        pltpu.make_async_copy(partial.at[0], partial.at[0], part_send).wait()

    pltpu.make_async_copy(squares, squares, sq_recv).wait()
    mean = (squared + jnp.sum(squares[...], axis=0)[:, :1]) / D
    inverse = lax.rsqrt(mean + 1e-6)
    normed_ref[...] = (scaled * inverse).astype(jnp.bfloat16)

    pltpu.make_async_copy(squares, squares, sq_send).wait()


def finish(stream_ref, normed_ref, stream_hbm, normed_hbm, sem):
    copies = [
        pltpu.make_async_copy(stream_ref, stream_hbm, sem.at[0]),
        pltpu.make_async_copy(normed_ref, normed_hbm, sem.at[1]),
    ]
    for copy in copies:
        copy.start()
    for copy in copies:
        copy.wait()


def local(
    queries,
    fresh_key_heads,
    fresh_value_heads,
    cached_keys,
    value_cache_rows,
    lengths,
    residual,
    sectioned_rows,
    owners,
    norm_gain,
):
    anywhere = pl.BlockSpec(memory_space=pl.ANY)
    bf16, f32 = jnp.bfloat16, jnp.float32
    outs = pl.pallas_call(
        kernel,
        out_shape=(pltpu.VMEM((SEQS, SLICE), bf16),) * 2,
        in_specs=[anywhere] * 10,
        out_specs=(pl.BlockSpec(memory_space=pltpu.VMEM),) * 2,
        scratch_shapes=[
            pltpu.VMEM((SEQS, HEADS * HEAD_SIZE), bf16),
            pltpu.VMEM((SEQS, HEAD_SIZE), bf16),
            pltpu.VMEM((SEQS, HEAD_SIZE), bf16),
            pltpu.SMEM((SEQS,), jnp.int32),
            pltpu.VMEM((SEQS, SLICE), bf16),
            pltpu.SMEM((BATCH,), jnp.int32),
            pltpu.VMEM((SLICE,), bf16),
            pltpu.VMEM((SEQS, SPAN, HEAD_SIZE), bf16),
            pltpu.VMEM((SEQS, SPAN, HEAD_SIZE), bf16),
            pltpu.VMEM((SEQS * HEADS, HEAD_SIZE), f32),
            pltpu.VMEM((SEQS, HEADS, SPAN), bf16),
            pltpu.VMEM((2 * SEQS * HEADS, HEAD_SIZE), f32),
            pltpu.VMEM((HEADS * 4, 8, 128), jnp.int32),
            pltpu.VMEM((CLANS, 8, 128), bf16),
            pltpu.VMEM((BATCH, 8, 128), bf16),
            pltpu.VMEM((PIECE, D), bf16),
            pltpu.VMEM((GROUP, PIECE, SLICE), bf16),
            pltpu.VMEM((BATCH, SEQS, SLICE), bf16),
            pltpu.VMEM((BATCH, SEQS, SLICE), bf16),
            pltpu.VMEM((SEQS, 128), f32),
            pltpu.VMEM((TENSOR - 1, SEQS, 128), f32),
            pltpu.SemaphoreType.DMA((7,)),
            pltpu.SemaphoreType.DMA,
            pltpu.SemaphoreType.DMA((SEQS,)),
            pltpu.SemaphoreType.DMA((SEQS,)),
        ]
        + [pltpu.SemaphoreType.DMA] * 3
        + [pltpu.SemaphoreType.DMA((BATCH // PART,))]
        + [pltpu.SemaphoreType.DMA] * 4,
        compiler_params=pltpu.CompilerParams(
            collective_id=0, has_side_effects=True, vmem_limit_bytes=56 * 1024 * 1024
        ),
    )(
        queries,
        fresh_key_heads,
        fresh_value_heads,
        cached_keys,
        value_cache_rows,
        lengths,
        residual,
        sectioned_rows,
        owners,
        norm_gain,
    )
    block = jax.ShapeDtypeStruct((SEQS, SLICE), bf16)
    return pl.pallas_call(
        finish,
        out_shape=(block, block),
        in_specs=[pl.BlockSpec(memory_space=pltpu.VMEM)] * 2,
        out_specs=(anywhere, anywhere),
        scratch_shapes=[pltpu.SemaphoreType.DMA((2,))],
    )(*[pltpu.with_memory_space_constraint(x, pltpu.VMEM) for x in outs])
    block = jax.ShapeDtypeStruct((SEQS, SLICE), bf16)


def solution(mesh):
    return jax.shard_map(
        local,
        mesh=mesh,
        in_specs=(
            P("batch", "tensor"),
            P("batch", "tensor"),
            P("batch", "tensor"),
            P("batch", "tensor", None, None),
            P("batch", "tensor", None, None),
            P("batch"),
            P("batch", "tensor"),
            P("batch", "tensor", None),
            P(),
            P("tensor"),
        ),
        out_specs=(P("batch", "tensor"), P("batch", "tensor")),
        check_vma=False,
    )
```
